512 devices in a mesh: gx: 32 (over y, z_lo, core), gy: 16 (over x, z_hi).
Axes of the slice: x: 4, y: 4, z: 16 (z_hi: 4, z_lo: 4; z = z_hi * 4 + z_lo), core: 2. Of those that a mesh axis runs over, the one named last changes fastest.
Arguments:
- positions: float32 [32, 16, 3, 2048], P('gx', 'gy'), may hold values from 0 to 6
- velocities: float32 [32, 16, 3, 2048], P('gx', 'gy'), may hold values from -6 to 6
- species: int32 [32, 16, 2048], P('gx', 'gy'), may hold values from 0 to 4
- masses: float32 [5], replicated, may hold values from 0.02 to 0.32
- centers: int32 [32, 16, 4096], P('gx', 'gy'), may hold values from 0 to 2047
- neighbours: int32 [32, 16, 4096], P('gx', 'gy'), may hold values from 0 to 10239, as said below
- edge_count: int32 [32, 16], P('gx', 'gy'), may hold values from 1536 to 4096, as said below
- ghost_list: int32 [32, 16, 1024], P('gx', 'gy'), may hold values from 0 to 2047, as said below
- mig_list: int32 [32, 16, 8, 64], P('gx', 'gy'), may hold values from 0 to 2047, as said below
- mig_count: int32 [32, 16, 8], P('gx', 'gy'), may hold values from 1 to 64, as said below
- w_rbf: bfloat16 [128, 8], replicated, may hold values from -2 to 2
- embed_center: bfloat16 [128, 5], replicated, may hold values from -3 to 3
- embed_neighbour: bfloat16 [128, 5], replicated, may hold values from -3 to 3
- w_mid: bfloat16 [2, 128, 128], replicated, may hold values from -0.5 to 0.5
- w_out: bfloat16 [128], replicated, may hold values from -0.5 to 0.5
Outputs:
- atom_energy: float32 [32, 16, 2048], P('gx', 'gy')
- forces: float32 [32, 16, 3, 2048], P('gx', 'gy')
- new_state: float32 [32, 16, 7, 2560], P('gx', 'gy')
The draws below stay inside these ranges and needn't reach their ends.
Inputs may be any that keep to these rules, and one draw needn't show every extreme that they name: `neighbours`: indices below 2048 name own atoms; index 2048 + k * 1024 + t names entry t of ghost_list of the neighbour at offset k. `edge_count`: a multiple of 128; some domain holds 4096 live edges. `ghost_list`: distinct own atoms within each domain. `mig_list`: all entries of one domain are distinct atoms. `mig_count`: every domain fills all 64 slots toward at least one neighbour.
All inputs are finite; a program needn't handle non-finite values.
Results may differ from the reference program's by a relative error of at most 0.024.
Values sent between devices are 32-bit elements; how exact they have to be, the bound alone decides.
A program may use at most 64 MiB of HBM per device.

```python
import math
import jax
import jax.numpy as jnp
from jax import lax

ATOMS = 2048
GHOSTS = 1024
EDGES = 4096
MIG = 64
WIDTH = 128
NBASIS = 8
SPECIES = 5
LAYERS = 2
DOMAINS_X = 32
DOMAINS_Y = 16


def draw_neighbours(key, part):
    key = jax.random.fold_in(key, 11)
    first, second, third, fourth = jax.random.split(key, 4)
    shape = (DOMAINS_X, DOMAINS_Y, EDGES)
    own = jax.random.randint(first, shape, 0, ATOMS)
    lent = jax.random.randint(second, shape, ATOMS, ATOMS + 8 * GHOSTS)
    coin = jax.random.randint(third, shape, 0, 2)
    picked = jnp.where(coin == 1, own, lent)
    spot = jax.random.randint(fourth, (DOMAINS_X, DOMAINS_Y, 1), 0, EDGES)
    marked = jnp.arange(EDGES)[None, None, :] == spot
    return jnp.where(marked, ATOMS + 8 * GHOSTS - 1, picked).astype(jnp.int32)


def draw_edge_count(key, part):
    key = jax.random.fold_in(key, 23)
    first, second = jax.random.split(key)
    lowest = max(1, EDGES // 320)
    blocks = jax.random.randint(first, (DOMAINS_X * DOMAINS_Y,), lowest, EDGES // 128 + 1)
    fullest = jax.random.randint(second, (), 0, DOMAINS_X * DOMAINS_Y)
    blocks = jnp.where(jnp.arange(DOMAINS_X * DOMAINS_Y) == fullest, EDGES // 128, blocks)
    return (blocks * 128).reshape(DOMAINS_X, DOMAINS_Y).astype(jnp.int32)


def draw_ghost_list(key, part):
    key = jax.random.fold_in(key, 37)
    keys = jax.random.split(key, DOMAINS_X * DOMAINS_Y)
    chosen = jax.vmap(lambda k: jax.random.permutation(k, ATOMS)[:GHOSTS])(keys)
    return chosen.reshape(DOMAINS_X, DOMAINS_Y, GHOSTS).astype(jnp.int32)


def draw_mig_list(key, part):
    key = jax.random.fold_in(key, 41)
    keys = jax.random.split(key, DOMAINS_X * DOMAINS_Y)
    chosen = jax.vmap(lambda k: jax.random.permutation(k, ATOMS)[:8 * MIG])(keys)
    return chosen.reshape(DOMAINS_X, DOMAINS_Y, 8, MIG).astype(jnp.int32)


def draw_mig_count(key, part):
    key = jax.random.fold_in(key, 53)
    first, second = jax.random.split(key)
    counts = jax.random.randint(first, (DOMAINS_X, DOMAINS_Y, 8), 1, MIG + 1)
    spot = jax.random.randint(second, (DOMAINS_X, DOMAINS_Y, 1), 0, 8)
    return jnp.where(jnp.arange(8)[None, None, :] == spot, MIG, counts).astype(jnp.int32)


def set_ends(values, key, low, top_value):
    longest = values.shape.index(max(values.shape))
    spots = []
    for shift in (0, 1):
        where = [jax.random.randint(jax.random.fold_in(key, axis), (), 0, length) for axis, length in enumerate(values.shape)]
        where[longest] = (where[longest] + shift) % values.shape[longest]
        spots.append(tuple(where))
    return values.at[spots[0]].set(low).at[spots[1]].set(top_value)


def steps_of(stream_key, shape, shards, low, high):
    def one(dim, blocks):
        heights = jax.random.uniform(jax.random.fold_in(jax.random.fold_in(stream_key, 6), dim), (blocks,), jnp.float32, low / len(shards), high / len(shards))
        return jnp.repeat(jnp.exp(heights), shape[dim] // blocks).reshape((-1,) + (1,) * (len(shape) - dim - 1))

    loudness = one(*shards[0])
    for cut in shards[1:]:
        loudness = loudness * one(*cut)
    return loudness


def centred(own_key, shape, scale, reach, shards=(), held_as=jnp.bfloat16):
    values = scale * jax.random.normal(own_key, shape, jnp.float32)
    if shards:
        values = values * steps_of(own_key, shape, shards, -0.22, 0.18)
    return jnp.clip(values, -reach, reach).astype(held_as)


def setup_inputs(seed: int = 0) -> dict:
    key_list = jax.random.split(jax.random.key(seed), 16)
    positions = jnp.clip(6.0 * jax.random.uniform(key_list[0], (DOMAINS_X, DOMAINS_Y, 3, ATOMS), jnp.float32) ** steps_of(key_list[0], (DOMAINS_X, DOMAINS_Y, 3, ATOMS), ((0, 32), (1, 16)), -0.2, 0.2), 0.0, 6.0)
    velocities = centred(key_list[1], (DOMAINS_X, DOMAINS_Y, 3, ATOMS), 1.0, 6.0, ((0, 32), (1, 16)), jnp.float32)
    species = set_ends(jax.random.randint(key_list[2], (DOMAINS_X, DOMAINS_Y, ATOMS), 0, SPECIES), jax.random.fold_in(key_list[2], 1), 0, SPECIES - 1).astype(jnp.int32)
    masses = jnp.clip(jnp.exp(jax.random.uniform(key_list[3], (SPECIES,), jnp.float32, math.log(0.02), math.log(0.32))), 0.02, 0.32)
    centers = set_ends(jax.random.randint(key_list[4], (DOMAINS_X, DOMAINS_Y, EDGES), 0, ATOMS), jax.random.fold_in(key_list[4], 1), 0, ATOMS - 1).astype(jnp.int32)
    neighbours = draw_neighbours(jax.random.fold_in(key_list[15], 71), 0)
    edge_count = draw_edge_count(jax.random.fold_in(key_list[15], 71), 0)
    ghost_list = draw_ghost_list(jax.random.fold_in(key_list[15], 71), 0)
    mig_list = draw_mig_list(jax.random.fold_in(key_list[15], 71), 0)
    mig_count = draw_mig_count(jax.random.fold_in(key_list[15], 71), 0)
    w_rbf = centred(key_list[10], (WIDTH, NBASIS), NBASIS ** -0.5, 2.0)
    embed_center = centred(key_list[11], (WIDTH, SPECIES), 0.6, 3.0)
    embed_neighbour = centred(key_list[12], (WIDTH, SPECIES), 0.6, 3.0)
    w_mid = centred(key_list[13], (LAYERS, WIDTH, WIDTH), WIDTH ** -0.5, 0.5)
    w_out = centred(key_list[14], (WIDTH,), WIDTH ** -0.5, 0.5)
    return {"positions": positions, "velocities": velocities, "species": species, "masses": masses, "centers": centers, "neighbours": neighbours, "edge_count": edge_count, "ghost_list": ghost_list, "mig_list": mig_list, "mig_count": mig_count, "w_rbf": w_rbf, "embed_center": embed_center, "embed_neighbour": embed_neighbour, "w_mid": w_mid, "w_out": w_out}


BOX_SIDE = 6.0
TIME_STEP = 0.1
OFFSETS = ((-1, -1), (-1, 0), (-1, 1), (0, -1), (0, 1), (1, -1), (1, 0), (1, 1))

def offset_column(first, second, height):
    values = [first * BOX_SIDE, second * BOX_SIDE] + [0.0] * (height - 2)
    return jnp.array(values, dtype=jnp.float32)[:, None]

def empty_column():
    return jnp.array([0.0] * 6 + [-1.0], dtype=jnp.float32)[:, None]

def edge_energy(delta, spec_center, spec_other, w_rbf, embed_center, embed_neighbour, w_mid, w_out):
    root = jnp.sqrt(lax.optimization_barrier(jnp.sum(delta * delta, axis=0)) + 1.0)
    nbasis = w_rbf.shape[1]
    freqs = (jnp.arange(nbasis).astype(jnp.float32) + 1.0) * (jnp.pi / 2.0)
    radial = (jnp.sin(freqs[:, None] * root[None, :]) / root[None, :]).astype(jnp.bfloat16)
    kinds = jnp.arange(embed_center.shape[1]).astype(jnp.float32)[:, None]
    onehot_center = (spec_center[None, :] == kinds).astype(jnp.bfloat16)
    onehot_other = (spec_other[None, :] == kinds).astype(jnp.bfloat16)
    hidden = jnp.dot(w_rbf, radial, preferred_element_type=jnp.float32)
    hidden = hidden + jnp.dot(embed_center, onehot_center, preferred_element_type=jnp.float32)
    hidden = hidden + jnp.dot(embed_neighbour, onehot_other, preferred_element_type=jnp.float32)
    active = jax.nn.silu(hidden).astype(jnp.bfloat16)
    for layer in range(w_mid.shape[0]):
        active = jax.nn.silu(jnp.dot(w_mid[layer], active, preferred_element_type=jnp.float32)).astype(jnp.bfloat16)
    return jnp.dot(w_out, active, preferred_element_type=jnp.float32)

def edge_terms(pos_center, pos_other, spec_center, spec_other, live, weights):
    delta = pos_other - pos_center

    def energy_of(moved):
        return edge_energy(moved, spec_center, spec_other, *weights)
    energies, pullback = jax.vjp(energy_of, delta)
    slope, = pullback(live)
    return (energies * live, slope)

def domain_work(pos_table, spec_table, centers, neighbours, count, atoms, weights):
    live = (jnp.arange(centers.shape[0]) < count).astype(jnp.float32)
    pos_center = jnp.take(pos_table, centers, axis=1)
    pos_other = jnp.take(pos_table, neighbours, axis=1)
    spec_center = jnp.take(spec_table, centers, axis=0)
    spec_other = jnp.take(spec_table, neighbours, axis=0)
    energies, slope = edge_terms(pos_center, pos_other, spec_center, spec_other, live, weights)
    energy = jnp.zeros((atoms,), jnp.float32).at[centers].add(energies)
    force_table = jnp.zeros(pos_table.shape, jnp.float32).at[:, centers].add(slope).at[:, neighbours].add(-slope)
    return (energy, force_table)

def reference(positions, velocities, species, masses, centers, neighbours, edge_count, ghost_list, mig_list, mig_count, w_rbf, embed_center, embed_neighbour, w_mid, w_out):
    weights = (w_rbf, embed_center, embed_neighbour, w_mid, w_out)
    spec_float = species.astype(jnp.float32)
    payload = jnp.concatenate([positions, spec_float[:, :, None, :]], axis=2)
    picks = jnp.broadcast_to(ghost_list[:, :, None, :], (DOMAINS_X, DOMAINS_Y, 4, GHOSTS))
    boundary = jnp.take_along_axis(payload, picks, axis=3)
    pieces = [payload]
    for first, second in OFFSETS:
        pieces.append(jnp.roll(boundary, (-first, -second), axis=(0, 1)) + offset_column(first, second, 4))
    table = jnp.concatenate(pieces, axis=3)
    width = ATOMS + 8 * GHOSTS
    flat_table = table.reshape(DOMAINS_X * DOMAINS_Y, 4, width)

    def per_domain(items):
        tab, cen, nei, cnt = items
        return domain_work(tab[:3], tab[3], cen, nei, cnt, ATOMS, weights)
    energy, force_table = lax.map(per_domain, (flat_table, centers.reshape(-1, EDGES), neighbours.reshape(-1, EDGES), edge_count.reshape(-1)))
    energy = energy.reshape(DOMAINS_X, DOMAINS_Y, ATOMS)
    force_table = force_table.reshape(DOMAINS_X, DOMAINS_Y, 3, width)
    own = force_table[..., :ATOMS]
    ghost_part = force_table[..., ATOMS:].reshape(DOMAINS_X, DOMAINS_Y, 3, 8, GHOSTS)
    returned = jnp.zeros((DOMAINS_X, DOMAINS_Y, 3, GHOSTS), jnp.float32)
    for index, (first, second) in enumerate(OFFSETS):
        returned = returned + jnp.roll(ghost_part[:, :, :, index], (first, second), axis=(0, 1))
    forces = jax.vmap(jax.vmap(lambda f, l, v: f.at[:, l].add(v)))(own, ghost_list, returned)
    inverse = jnp.take(1.0 / masses, species, axis=0)
    velocity_new = velocities + TIME_STEP * forces * inverse[:, :, None, :]
    position_new = positions + TIME_STEP * velocity_new
    state = jnp.concatenate([position_new, velocity_new, spec_float[:, :, None, :]], axis=2)
    slots = jnp.arange(MIG)
    valid = slots[None, None, None, :] < mig_count[..., None]
    blocks = []
    for index, (first, second) in enumerate(OFFSETS):
        picks = jnp.broadcast_to(mig_list[:, :, None, index, :], (DOMAINS_X, DOMAINS_Y, 7, MIG))
        rows = jnp.take_along_axis(state, picks, axis=3) + offset_column(-first, -second, 7)
        rows = jnp.where(valid[:, :, None, index, :], rows, empty_column())
        blocks.append(jnp.roll(rows, (first, second), axis=(0, 1)))

    def leaving(lists, flags):
        return jnp.zeros((ATOMS,), jnp.float32).at[lists.reshape(-1)].max(flags.reshape(-1).astype(jnp.float32))
    gone = jax.vmap(jax.vmap(leaving))(mig_list, valid)
    kept = jnp.where(gone[:, :, None, :] > 0.0, empty_column(), state)
    new_state = jnp.concatenate([kept] + blocks, axis=3)
    return (energy, forces, new_state)
```

```python
import functools

import jax
import jax.numpy as jnp
from jax import lax
from jax.experimental import pallas as pl
from jax.experimental.pallas import tpu as pltpu
from jax.sharding import PartitionSpec as P

BOX_SIDE = 6.0
TIME_STEP = 0.1
OFFSETS = ((-1, -1), (-1, 0), (-1, 1), (0, -1), (0, 1), (1, -1), (1, 0), (1, 1))

ATOMS = 2048
GHOSTS = 1024
EDGES = 4096
MIG = 64
LO = 256
OWN_HI = ATOMS // LO
GHOST_HI = GHOSTS // LO
ALL_HI = OWN_HI + 8 * GHOST_HI
CHUNK = 512
MESH = pl.DeviceIdType.MESH
F32 = jnp.float32
BF16 = jnp.bfloat16


def dot(a, b):
    return jnp.dot(a, b, preferred_element_type=F32)


def dot_nt(a, b):
    return lax.dot_general(a, b, (((1,), (1,)), ((), ())), preferred_element_type=F32)


def iota(shape, dim):
    return lax.broadcasted_iota(jnp.int32, shape, dim)


def tall(row, height):
    return jnp.broadcast_to(row, (height, row.shape[1]))


def split_rows(both):
    head = both.astype(BF16).astype(F32)
    return jnp.where(iota(both.shape, 0) < 4, head, both - head)


def join_rows(both):
    return both + pltpu.roll(both, 4, 0)


def write_onehot(ref, cols, low, rows):
    low16 = tall(low, 16).astype(F32).astype(BF16)
    one = jnp.ones(low16.shape, BF16)
    zero = jnp.zeros(low16.shape, BF16)
    for i in range(LO // 16):
        span = pl.ds(16 * i, 16)
        ref[span, cols] = jnp.where(rows[span, 0 : low.shape[1]] == low16, one, zero)


def masked_rows(high16, values16, count):
    first = (iota(values16.shape, 0) >= 8).astype(F32)
    zero = jnp.zeros(values16.shape, BF16)
    return jnp.concatenate(
        [
            jnp.where(high16 == (first + float(2 * i)).astype(BF16), values16, zero)
            for i in range(count // 2)
        ],
        axis=0,
    )


def pick_rows(product, high, first, total, height=8):
    for h in range(product.shape[0] // height):
        total = jnp.where(high == first + h, product[height * h : height * (h + 1)], total)
    return total


def doubled(value):
    return jnp.concatenate([value, value], axis=0)


def kernel(
    nx, ny,
    pos, vel, spec, mass, cen, nei, count, ghost, mig_list, mig_count,
    w_rbf, emb_c, emb_n, w_mid, w_out,
    energy_out, force_out, state_out,
    rows_ref, pay, tab_own, tab_ghost, hot_c, hot_n, hot_g, hot_m, sel_c, sel_n,
    acc_c, acc_n, lend, ghosts, back, back_in, ring, ring_in, step_ref, speeds, state, gone, lists, mig_out, mig_in, sum_c, sum_n,
    send_sem, recv_sem,
):
    i = lax.axis_index("gx")
    j = lax.axis_index("gy")

    def device(first, second):
        return (lax.rem(i + first + nx, nx), lax.rem(j + second + ny, ny))

    def remote(src, dst, sem, first, second):
        return pltpu.make_async_remote_copy(
            src_ref=src, dst_ref=dst, send_sem=send_sem.at[sem], recv_sem=recv_sem.at[sem],
            device_id=device(first, second), device_id_type=MESH,
        )

    barrier = pltpu.get_barrier_semaphore()
    for first, second in OFFSETS:
        pl.semaphore_signal(barrier, inc=1, device_id=device(first, second), device_id_type=MESH)

    rows_ref[...] = iota(rows_ref.shape, 0).astype(F32).astype(BF16)
    spec_row = spec[0].astype(F32)
    for r in range(3):
        pay[r : r + 1, :] = pos[0, r]
        pay[r + 4 : r + 5, :] = pos[0, r]
    pay[3:4, :] = spec_row
    pay[7:8, :] = spec_row
    both = split_rows(pay[...])
    for h in range(0, OWN_HI, 2):
        tab_own[8 * h : 8 * h + 16, :] = jnp.concatenate(
            [both[:, LO * h : LO * (h + 1)], both[:, LO * (h + 1) : LO * (h + 2)]], axis=0
        ).astype(BF16)
    lent = ghost[0]
    write_onehot(hot_g, pl.ds(0, GHOSTS), lent & (LO - 1), rows_ref)
    lent_high = tall(lent // LO, 8)
    picked = pick_rows(dot(tab_own[...], hot_g[...]), lent_high, 0, jnp.zeros((8, GHOSTS), F32))
    lend[...] = join_rows(picked)[0:4]

    pl.semaphore_wait(barrier, 8)

    to_y = [remote(lend, ghosts.at[1, 1 - s], n, 0, s) for n, s in enumerate((-1, 1))]
    for copy in to_y:
        copy.start()
    to_x = [
        [remote(lend if b == 0 else ghosts.at[1, 1 + b], ghosts.at[1 - s, 1 + b], 2 + 3 * n + m, s, 0) for n, s in enumerate((-1, 1))]
        for m, b in enumerate((0, -1, 1))
    ]
    for copy in to_x[0]:
        copy.start()

    def own_chunk(step, carry):
        cols = pl.ds(pl.multiple_of(step * CHUNK, CHUNK), CHUNK)
        for index, hot, sel, acc in ((cen, hot_c, sel_c, acc_c), (nei, hot_n, sel_n, acc_n)):
            place = index[0, :, cols]
            write_onehot(hot, cols, place & (LO - 1), rows_ref)
            high = tall(place // LO, 8)
            sel[:, cols] = high
            acc[:, cols] = pick_rows(dot(tab_own[...], hot[:, cols]), high, 0, jnp.zeros((8, CHUNK), F32))
        return carry

    for n, s in enumerate((-1, 1)):
        to_y[n].wait_recv()
    for m in (1, 2):
        for copy in to_x[m]:
            copy.start()
    lax.fori_loop(0, EDGES // CHUNK, own_chunk, 0)

    inverse = jnp.zeros((1, ATOMS), F32)
    for kind in range(5):
        inverse = jnp.where(spec_row == float(kind), 1.0 / jnp.full((1, ATOMS), mass[kind], F32), inverse)
    step_ref[...] = TIME_STEP * tall(inverse, 8)
    for r in range(3):
        speeds[r : r + 1, :] = vel[0, r]
    state[...] = jnp.zeros(state.shape, F32)
    state[6:7, :] = spec_row
    lists[...] = jnp.zeros(lists.shape, jnp.int32)
    lists[:, 0:MIG] = mig_list[0, 0]
    listed = lists[...]
    moved = pltpu.roll(listed, MIG, 1)
    lane = iota((1, 2 * MIG), 1)
    mig_high = []
    mig_shift = []
    mig_valid = []
    for pair in range(4):
        place = jnp.where(lane < MIG, listed[2 * pair : 2 * pair + 1], moved[2 * pair + 1 : 2 * pair + 2])
        write_onehot(hot_m, pl.ds(2 * MIG * pair, 2 * MIG), place & (LO - 1), rows_ref)
        mig_high.append(place // LO)
        limit = jnp.where(lane < MIG, mig_count[0, 0, 2 * pair], mig_count[0, 0, 2 * pair + 1] + MIG)
        mig_valid.append((lane < limit).astype(F32))
        row = iota((8, 2 * MIG), 0)
        half = iota((8, 2 * MIG), 1) < MIG
        (a0, b0), (a1, b1) = OFFSETS[2 * pair], OFFSETS[2 * pair + 1]
        mig_shift.append(
            jnp.where(row == 0, jnp.where(half, -BOX_SIDE * a0, -BOX_SIDE * a1), 0.0)
            + jnp.where(row == 1, jnp.where(half, -BOX_SIDE * b0, -BOX_SIDE * b1), 0.0)
        )
    mig_high = jnp.concatenate(mig_high, axis=1)
    mig_shift = jnp.concatenate(mig_shift, axis=1)
    mig_valid = jnp.concatenate(mig_valid, axis=1)
    leaving = masked_rows(
        tall(mig_high, 16).astype(F32).astype(BF16), tall(mig_valid, 16).astype(BF16), OWN_HI
    )
    left = dot_nt(leaving, hot_m[...])
    for h in range(OWN_HI):
        gone[:, LO * h : LO * (h + 1)] = left[8 * h : 8 * h + 8]

    def eight(weights):
        values = weights.astype(F32)
        short = 8 - values.shape[0]
        return jnp.concatenate([values, jnp.zeros((short, values.shape[1]), F32)], axis=0) if short else values

    rbf = 0.5 * w_rbf[...].astype(F32)
    w_in = jnp.concatenate([rbf, 0.5 * eight(emb_c[...]), 0.5 * eight(emb_n[...]), jnp.zeros(rbf.shape, F32)], axis=0).T.astype(BF16)
    mid = [w_mid[layer].astype(F32) for layer in range(2)]
    half_mid = [(0.5 * w).astype(BF16) for w in mid]
    out_row = w_out[...].astype(F32)
    out_rows = tall(out_row, 8).astype(BF16)
    back_1 = (0.5 * mid[1].T * out_row).astype(BF16)
    back_0 = (0.5 * mid[0].T).astype(BF16)
    back_in_w = rbf.astype(BF16)

    for copy in [c for pair in to_x for c in pair]:
        copy.wait_recv()
    for k, (first, second) in enumerate(OFFSETS):
        both = split_rows(doubled(ghosts[1 + first, 1 + second]))
        for c in range(0, GHOST_HI, 2):
            at = 8 * (GHOST_HI * k + c)
            tab_ghost[at : at + 16, :] = jnp.concatenate(
                [both[:, LO * c : LO * (c + 1)], both[:, LO * (c + 1) : LO * (c + 2)]], axis=0
            ).astype(BF16)

    live_edges = count[0, 0]

    def edge_chunk(step, carry):
        start = pl.multiple_of(step * CHUNK, CHUNK)
        cols = pl.ds(start, CHUNK)
        shape = (8, CHUNK)
        row = iota(shape, 0)
        high_n = sel_n[:, cols]
        high_c = sel_c[:, cols]
        other = pick_rows(dot(tab_ghost[...], hot_n[:, cols]), high_n, OWN_HI, acc_n[:, cols])
        other = join_rows(other)
        centre = join_rows(acc_c[:, cols])
        block = (high_n - OWN_HI) // GHOST_HI
        cell = block + (block >= 4).astype(jnp.int32)
        third = (cell * 11) >> 5
        side = jnp.where(row & 3 == 0, third - 1, jnp.where(row & 3 == 1, cell - 3 * third - 1, 0))
        side = jnp.where(high_n < OWN_HI, 0, side)
        delta = other - centre + BOX_SIDE * side.astype(F32)
        square = jnp.sum(jnp.where(row < 3, delta * delta, 0.0), axis=0, keepdims=True) + 1.0
        q = tall(jnp.sqrt(square), 8)
        inv_q = 1.0 / q
        freq = (row + 1).astype(F32)
        phase = freq * q
        turn = jnp.floor(phase + 0.5)
        x = (phase - turn) * (jnp.pi / 2)
        x2 = x * x
        sine = x * (1.0 + x2 * (-1.0 / 6 + x2 * (1.0 / 120 + x2 * (-1.0 / 5040 + x2 * (1.0 / 362880)))))
        cosine = 1.0 + x2 * (-0.5 + x2 * (1.0 / 24 + x2 * (-1.0 / 720 + x2 * (1.0 / 40320))))
        quarter = turn.astype(jnp.int32)
        odd = (quarter & 1) == 1
        sign = (1 - (quarter & 2)).astype(F32)
        sin_p = jnp.where(odd, cosine, sine) * sign
        cos_p = jnp.where(odd, -sine, cosine) * sign
        radial = sin_p * inv_q
        kind_c = tall(centre[3:4], 8)
        kind_n = tall(other[3:4], 8)
        kinds = row.astype(F32)
        features = jnp.concatenate(
            [radial, (kind_c == kinds).astype(F32), (kind_n == kinds).astype(F32), jnp.zeros(shape, F32)], axis=0
        ).astype(BF16)

        def active(half):
            t = jnp.tanh(half)
            p = 1.0 + t
            a = half * p
            return a.astype(BF16), p + a * (1.0 - t)

        act_0, slope_0 = active(dot(w_in, features))
        act_1, slope_1 = active(dot(half_mid[0], act_0))
        act_2, slope_2 = active(dot(half_mid[1], act_1))
        energy = dot(out_rows, act_2)
        cot_1 = (dot(back_1, slope_2.astype(BF16)) * slope_1).astype(BF16)
        cot_0 = (dot(back_0, cot_1) * slope_0).astype(BF16)
        grad = dot(back_in_w, cot_0)
        pull = grad * ((jnp.pi / 2) * freq * cos_p - radial) * inv_q
        pull = tall(jnp.sum(pull, axis=0, keepdims=True), 8) * inv_q
        live = (start + iota(shape, 1) < live_edges).astype(F32)
        values = jnp.where(row & 3 == 3, energy, delta * pull) * live
        values16 = doubled(split_rows(values)).astype(BF16)
        high_c16 = doubled(high_c.astype(F32)).astype(BF16)
        high_n16 = doubled(high_n.astype(F32)).astype(BF16)
        sum_c[...] += dot_nt(masked_rows(high_c16, values16, OWN_HI), hot_c[:, cols])
        sum_n[...] += dot_nt(masked_rows(high_n16, values16, ALL_HI), hot_n[:, cols])
        return carry

    sum_c[...] = jnp.zeros(sum_c.shape, F32)
    sum_n[...] = jnp.zeros(sum_n.shape, F32)
    lax.fori_loop(0, EDGES // CHUNK, edge_chunk, 0)

    def parts(k, c):
        at = 8 * (OWN_HI + GHOST_HI * k + c)
        return -join_rows(sum_n[at : at + 8, :])[0:4]

    for k, (first, second) in enumerate(OFFSETS):
        for c in range(GHOST_HI):
            span = slice(LO * c, LO * (c + 1))
            if first == 0:
                ring[(second + 1) // 2, :, span] = parts(k, c)
            else:
                back[(first + 1) // 2, second + 1, :, span] = parts(k, c)
    gx_back = [remote(back.at[n], back_in.at[n], 8 + n, s, 0) for n, s in enumerate((-1, 1))]
    for copy in gx_back:
        copy.start()

    own = []
    for h in range(OWN_HI):
        at = 8 * h
        centred = join_rows(sum_c[at : at + 8, :])
        energy_out[0, :, LO * h : LO * (h + 1)] = centred[3:4]
        own.append(centred - join_rows(sum_n[at : at + 8, :]))

    for copy in gx_back:
        copy.wait_recv()
    for n, b in enumerate((-1, 1)):
        ring[n] = ring[n] + back_in[0, 1 + b] + back_in[1, 1 + b]
    gy_back = [remote(ring.at[n], ring_in.at[n], 10 + n, 0, s) for n, s in enumerate((-1, 1))]
    for copy in gy_back:
        copy.start()
    returned = back_in[0, 1] + back_in[1, 1]
    for copy in gy_back:
        copy.wait_recv()
    returned = returned + ring_in[0] + ring_in[1]
    values16 = doubled(split_rows(doubled(returned))).astype(BF16)
    high16 = doubled(lent_high.astype(F32)).astype(BF16)
    added = dot_nt(masked_rows(high16, values16, OWN_HI), hot_g[...])

    for h in range(OWN_HI):
        span = slice(LO * h, LO * (h + 1))
        force = (own[h] + join_rows(added[8 * h : 8 * h + 8]))[0:3]
        for r in range(3):
            force_out[0, r, :, span] = force[r : r + 1]
        speed = speeds[0:3, span] + force * step_ref[0:3, span]
        state[0:3, span] = pay[0:3, span] + TIME_STEP * speed
        state[3:6, span] = speed
    table = []
    for h in range(OWN_HI):
        value = state[:, LO * h : LO * (h + 1)]
        head = value.astype(BF16)
        table += [value, value - head.astype(F32)]
    product = dot(jnp.concatenate(table, axis=0).astype(BF16), hot_m[...])
    chosen = pick_rows(product, tall(mig_high, 16), 0, jnp.zeros((16, 8 * MIG), F32), 16)
    empty = jnp.where(iota((8, 1), 0) == 6, -1.0, 0.0)
    leaving = jnp.where(tall(mig_valid, 8) > 0.0, chosen[0:8] + chosen[8:16] + mig_shift, empty)
    for pair in range(4):
        mig_out[pair] = leaving[:, 2 * MIG * pair : 2 * MIG * (pair + 1)]
    moves = [remote(mig_out.at[k // 2], mig_in.at[k], 12 + k, *OFFSETS[k]) for k in range(8)]
    for copy in moves:
        copy.start()
    kept = jnp.where(gone[...] > 0.0, empty, state[...])
    for r in range(7):
        state_out[0, r, :, 0:ATOMS] = kept[r : r + 1]
    for copy in moves:
        copy.wait_recv()
    for pair in range(4):
        arrived = jnp.where(iota((8, 2 * MIG), 1) < MIG, mig_in[2 * pair], mig_in[2 * pair + 1])
        for r in range(7):
            state_out[0, r, :, ATOMS + 2 * MIG * pair : ATOMS + 2 * MIG * (pair + 1)] = arrived[r : r + 1]
    for copy in to_y + [c for pair in to_x for c in pair] + gx_back + gy_back + moves:
        copy.wait_send()


def shards(
    positions, velocities, species, masses, centers, neighbours, edge_count, ghost_list, mig_list, mig_count,
    w_rbf, embed_center, embed_neighbour, w_mid, w_out,
):
    vmem = pl.BlockSpec(memory_space=pltpu.VMEM)
    smem = pl.BlockSpec(memory_space=pltpu.SMEM)
    rows_first = functools.partial(jnp.transpose, axes=(0, 2, 1, 3))
    energy, forces, new_state = pl.pallas_call(
        functools.partial(kernel, lax.axis_size("gx"), lax.axis_size("gy")),
        out_shape=(
            jax.ShapeDtypeStruct((1, 1, ATOMS), F32),
            jax.ShapeDtypeStruct((1, 3, 1, ATOMS), F32),
            jax.ShapeDtypeStruct((1, 7, 1, ATOMS + 8 * MIG), F32),
        ),
        in_specs=[vmem, vmem, vmem, smem, vmem, vmem, smem, vmem, vmem, smem] + [vmem] * 5,
        out_specs=(vmem, vmem, vmem),
        scratch_shapes=[
            pltpu.VMEM((LO, GHOSTS), BF16),
            pltpu.VMEM((8, ATOMS), F32),
            pltpu.VMEM((8 * OWN_HI, LO), BF16),
            pltpu.VMEM((64 * GHOST_HI, LO), BF16),
            pltpu.VMEM((LO, EDGES), BF16),
            pltpu.VMEM((LO, EDGES), BF16),
            pltpu.VMEM((LO, GHOSTS), BF16),
            pltpu.VMEM((LO, 8 * MIG), BF16),
            pltpu.VMEM((8, EDGES), jnp.int32),
            pltpu.VMEM((8, EDGES), jnp.int32),
            pltpu.VMEM((8, EDGES), F32),
            pltpu.VMEM((8, EDGES), F32),
            pltpu.VMEM((4, GHOSTS), F32),
            pltpu.VMEM((3, 3, 4, GHOSTS), F32),
            pltpu.VMEM((2, 3, 4, GHOSTS), F32),
            pltpu.VMEM((2, 3, 4, GHOSTS), F32),
            pltpu.VMEM((2, 4, GHOSTS), F32),
            pltpu.VMEM((2, 4, GHOSTS), F32),
            pltpu.VMEM((8, ATOMS), F32),
            pltpu.VMEM((8, ATOMS), F32),
            pltpu.VMEM((8, ATOMS), F32),
            pltpu.VMEM((8, ATOMS), F32),
            pltpu.VMEM((8, 2 * MIG), jnp.int32),
            pltpu.VMEM((4, 8, 2 * MIG), F32),
            pltpu.VMEM((8, 8, 2 * MIG), F32),
            pltpu.VMEM((8 * OWN_HI, LO), F32),
            pltpu.VMEM((8 * ALL_HI, LO), F32),
            pltpu.SemaphoreType.DMA((20,)),
            pltpu.SemaphoreType.DMA((20,)),
        ],
        compiler_params=pltpu.CompilerParams(
            collective_id=0, has_side_effects=True, vmem_limit_bytes=48 * 1024 * 1024
        ),
    )(
        rows_first(positions), rows_first(velocities), species, masses, centers, neighbours, edge_count, ghost_list,
        mig_list, mig_count, w_rbf.T, embed_center.T, embed_neighbour.T, w_mid, w_out.reshape(1, -1),
    )
    return (energy, rows_first(forces), rows_first(new_state))


def solution(mesh):
    return jax.shard_map(
        shards,
        mesh=mesh,
        in_specs=(
            P("gx", "gy", None, None),
            P("gx", "gy", None, None),
            P("gx", "gy", None),
            P(),
            P("gx", "gy", None),
            P("gx", "gy", None),
            P("gx", "gy"),
            P("gx", "gy", None),
            P("gx", "gy", None, None),
            P("gx", "gy", None),
            P(),
            P(),
            P(),
            P(),
            P(),
        ),
        out_specs=(P("gx", "gy", None), P("gx", "gy", None, None), P("gx", "gy", None, None)),
        check_vma=False,
    )
```

```python
import functools

import jax
import jax.numpy as jnp
from jax import lax
from jax.experimental import pallas as pl
from jax.experimental.pallas import tpu as pltpu
from jax.sharding import PartitionSpec as P

BOX_SIDE = 6.0
TIME_STEP = 0.1
NEAR = (1, 6, 3, 4)
FAR = (0, 2, 5, 7)
OFFSETS = ((-1, -1), (-1, 0), (-1, 1), (0, -1), (0, 1), (1, -1), (1, 0), (1, 1))

ATOMS = 2048
GHOSTS = 1024
EDGES = 4096
MIG = 64
LO = 256
OWN_HI = ATOMS // LO
GHOST_HI = GHOSTS // LO
ALL_HI = OWN_HI + 8 * GHOST_HI
CHUNK = 4096
MESH = pl.DeviceIdType.MESH
F32 = jnp.float32
BF16 = jnp.bfloat16


def dot(a, b):
    return jnp.dot(a, b, preferred_element_type=F32)


def dot_nt(a, b):
    return lax.dot_general(a, b, (((1,), (1,)), ((), ())), preferred_element_type=F32)


def iota(shape, dim):
    return lax.broadcasted_iota(jnp.int32, shape, dim)


def tall(row, height):
    return jnp.broadcast_to(row, (height, row.shape[1]))


def split_rows(both):
    head = both.astype(BF16).astype(F32)
    return jnp.where(iota(both.shape, 0) < 4, head, both - head)


def join_rows(both):
    return both + pltpu.roll(both, 4, 0)


def write_onehot(ref, cols, low, rows):
    low16 = tall(low, 16).astype(F32).astype(BF16)
    one = jnp.ones(low16.shape, BF16)
    zero = jnp.zeros(low16.shape, BF16)
    for i in range(LO // 16):
        span = pl.ds(16 * i, 16)
        ref[span, cols] = jnp.where(rows[span, 0 : low.shape[1]] == low16, one, zero)


def masked_rows(high16, values16, count):
    first = (iota(values16.shape, 0) >= 8).astype(F32)
    zero = jnp.zeros(values16.shape, BF16)
    return jnp.concatenate(
        [
            jnp.where(high16 == (first + float(2 * i)).astype(BF16), values16, zero)
            for i in range(count // 2)
        ],
        axis=0,
    )


def pick_rows(product, high, first, total, height=8):
    for h in range(product.shape[0] // height):
        total = jnp.where(high == first + h, product[height * h : height * (h + 1)], total)
    return total


def doubled(value):
    return jnp.concatenate([value, value], axis=0)


def kernel(
    nx, ny,
    *refs,
):
    inputs, outputs, local, refs = refs[:15], refs[15:18], refs[18:33], refs[33:]
    energy_out, force_out, state_out = outputs
    (
    rows_ref, pay, tab_own, tab_near, tab_far, hot_c, hot_n, hot_g, hot_m, sel_c, sel_n,
    acc_c, acc_n, lend, ghosts, back, back_in, step_ref, speeds, state, gone, lists, mig_out, mig_in, sum_c, sum_n,
    send_sem, recv_sem, load_sem,
    ) = refs
    pos, vel, spec, mass, cen, nei, count, ghost, mig_list, mig_count, w_rbf, emb_c, emb_n, w_mid, w_out = local
    i = lax.axis_index("gx")
    j = lax.axis_index("gy")

    def device(first, second):
        return (lax.rem(i + first + nx, nx), lax.rem(j + second + ny, ny))

    def remote(src, dst, sem, first, second):
        return pltpu.make_async_remote_copy(
            src_ref=src, dst_ref=dst, send_sem=send_sem.at[sem], recv_sem=recv_sem.at[sem],
            device_id=device(first, second), device_id_type=MESH,
        )

    barrier = pltpu.get_barrier_semaphore()
    for first, second in OFFSETS:
        pl.semaphore_signal(barrier, inc=1, device_id=device(first, second), device_id_type=MESH)

    loads = [pltpu.make_async_copy(inputs[n], local[n], load_sem.at[n]) for n in range(15)]
    first_loads, later_loads = (0, 2, 7), (4, 5, 1, 3, 6, 8, 9, 10, 11, 12, 13, 14)
    for n in first_loads + later_loads:
        loads[n].start()

    rows_ref[...] = iota(rows_ref.shape, 0).astype(F32).astype(BF16)
    for n in first_loads:
        loads[n].wait()
    spec_row = spec[0].astype(F32)
    for r in range(3):
        pay[r : r + 1, :] = pos[0, r]
        pay[r + 4 : r + 5, :] = pos[0, r]
    pay[3:4, :] = spec_row
    pay[7:8, :] = spec_row
    both = split_rows(pay[...])
    for h in range(0, OWN_HI, 2):
        tab_own[8 * h : 8 * h + 16, :] = jnp.concatenate(
            [both[:, LO * h : LO * (h + 1)], both[:, LO * (h + 1) : LO * (h + 2)]], axis=0
        ).astype(BF16)
    lent = ghost[0]
    write_onehot(hot_g, pl.ds(0, GHOSTS), lent & (LO - 1), rows_ref)
    lent_high = tall(lent // LO, 8)
    picked = pick_rows(dot(tab_own[...], hot_g[...]), lent_high, 0, jnp.zeros((8, GHOSTS), F32))
    lend[...] = join_rows(picked)[0:4]

    pl.semaphore_wait(barrier, 8)

    lends = [remote(lend, ghosts.at[k], k, *OFFSETS[7 - k]) for k in range(8)]
    for k in FAR + NEAR:
        lends[k].start()
    for n in later_loads:
        loads[n].wait()

    def own_chunk(step, carry):
        cols = pl.ds(pl.multiple_of(step * CHUNK, CHUNK), CHUNK)
        for index, hot, sel, acc in ((cen, hot_c, sel_c, acc_c), (nei, hot_n, sel_n, acc_n)):
            place = index[0, :, cols]
            write_onehot(hot, cols, place & (LO - 1), rows_ref)
            high = tall(place // LO, 8)
            sel[:, cols] = high
            acc[:, cols] = pick_rows(dot(tab_own[...], hot[:, cols]), high, 0, jnp.zeros((8, CHUNK), F32))
        return carry

    lax.fori_loop(0, EDGES // CHUNK, own_chunk, 0)

    inverse = jnp.zeros((1, ATOMS), F32)
    for kind in range(5):
        inverse = jnp.where(spec_row == float(kind), 1.0 / jnp.full((1, ATOMS), mass[kind], F32), inverse)
    step_ref[...] = TIME_STEP * tall(inverse, 8)
    for r in range(3):
        speeds[r : r + 1, :] = vel[0, r]
    state[...] = jnp.zeros(state.shape, F32)
    state[6:7, :] = spec_row
    lists[...] = jnp.zeros(lists.shape, jnp.int32)
    lists[:, 0:MIG] = mig_list[0, 0]
    listed = lists[...]
    moved = pltpu.roll(listed, MIG, 1)
    lane = iota((1, 2 * MIG), 1)
    mig_high = []
    mig_shift = []
    mig_valid = []
    for pair in range(4):
        place = jnp.where(lane < MIG, listed[2 * pair : 2 * pair + 1], moved[2 * pair + 1 : 2 * pair + 2])
        write_onehot(hot_m, pl.ds(2 * MIG * pair, 2 * MIG), place & (LO - 1), rows_ref)
        mig_high.append(place // LO)
        limit = jnp.where(lane < MIG, mig_count[0, 0, 2 * pair], mig_count[0, 0, 2 * pair + 1] + MIG)
        mig_valid.append((lane < limit).astype(F32))
        row = iota((8, 2 * MIG), 0)
        half = iota((8, 2 * MIG), 1) < MIG
        (a0, b0), (a1, b1) = OFFSETS[2 * pair], OFFSETS[2 * pair + 1]
        mig_shift.append(
            jnp.where(row == 0, jnp.where(half, -BOX_SIDE * a0, -BOX_SIDE * a1), 0.0)
            + jnp.where(row == 1, jnp.where(half, -BOX_SIDE * b0, -BOX_SIDE * b1), 0.0)
        )
    mig_high = jnp.concatenate(mig_high, axis=1)
    mig_shift = jnp.concatenate(mig_shift, axis=1)
    mig_valid = jnp.concatenate(mig_valid, axis=1)
    leaving = masked_rows(
        tall(mig_high, 16).astype(F32).astype(BF16), tall(mig_valid, 16).astype(BF16), OWN_HI
    )
    left = dot_nt(leaving, hot_m[...])
    for h in range(OWN_HI):
        gone[:, LO * h : LO * (h + 1)] = left[8 * h : 8 * h + 8]

    def eight(weights):
        values = weights.astype(F32)
        short = 8 - values.shape[0]
        return jnp.concatenate([values, jnp.zeros((short, values.shape[1]), F32)], axis=0) if short else values

    rbf = 0.5 * w_rbf[...].astype(F32)
    w_in = jnp.concatenate([rbf, 0.5 * eight(emb_c[...]), 0.5 * eight(emb_n[...]), jnp.zeros(rbf.shape, F32)], axis=0).T.astype(BF16)
    mid = [w_mid[layer].astype(F32) for layer in range(2)]
    half_mid = [(0.5 * w).astype(BF16) for w in mid]
    out_row = w_out[...].astype(F32)
    out_rows = tall(out_row, 8).astype(BF16)
    back_1 = (0.5 * mid[1].T * out_row).astype(BF16)
    back_0 = (0.5 * mid[0].T).astype(BF16)
    back_in_w = rbf.astype(BF16)

    def ghost_table(ref, blocks):
        for m, k in enumerate(blocks):
            lends[k].wait_recv()
            both = split_rows(doubled(ghosts[k]))
            for c in range(0, GHOST_HI, 2):
                at = 8 * (GHOST_HI * m + c)
                ref[at : at + 16, :] = jnp.concatenate(
                    [both[:, LO * c : LO * (c + 1)], both[:, LO * (c + 1) : LO * (c + 2)]], axis=0
                ).astype(BF16)

    def pick_ghosts(ref, blocks, cols, total):
        product = dot(ref[...], hot_n[:, cols])
        high = sel_n[:, cols]
        size = 8 * GHOST_HI
        for m, k in enumerate(blocks):
            total = pick_rows(product[size * m : size * (m + 1)], high, OWN_HI + GHOST_HI * k, total)
        return total

    def near_chunk(step, carry):
        cols = pl.ds(pl.multiple_of(step * CHUNK, CHUNK), CHUNK)
        acc_n[:, cols] = pick_ghosts(tab_near, NEAR, cols, acc_n[:, cols])
        return carry

    ghost_table(tab_near, NEAR)
    lax.fori_loop(0, EDGES // CHUNK, near_chunk, 0)
    ghost_table(tab_far, FAR)

    live_edges = count[0, 0, 0]

    def edge_chunk(step, carry):
        start = pl.multiple_of(step * CHUNK, CHUNK)
        cols = pl.ds(start, CHUNK)
        shape = (8, CHUNK)
        row = iota(shape, 0)
        high_n = sel_n[:, cols]
        high_c = sel_c[:, cols]
        other = pick_ghosts(tab_far, FAR, cols, acc_n[:, cols])
        other = join_rows(other)
        centre = join_rows(acc_c[:, cols])
        block = (high_n - OWN_HI) // GHOST_HI
        cell = block + (block >= 4).astype(jnp.int32)
        third = (cell * 11) >> 5
        side = jnp.where(row & 3 == 0, third - 1, jnp.where(row & 3 == 1, cell - 3 * third - 1, 0))
        side = jnp.where(high_n < OWN_HI, 0, side)
        delta = other - centre + BOX_SIDE * side.astype(F32)
        square = jnp.sum(jnp.where(row < 3, delta * delta, 0.0), axis=0, keepdims=True) + 1.0
        q = tall(jnp.sqrt(square), 8)
        inv_q = 1.0 / q
        freq = (row + 1).astype(F32)
        phase = freq * q
        turn = jnp.floor(phase + 0.5)
        x = (phase - turn) * (jnp.pi / 2)
        x2 = x * x
        sine = x * (1.0 + x2 * (-1.0 / 6 + x2 * (1.0 / 120 + x2 * (-1.0 / 5040 + x2 * (1.0 / 362880)))))
        cosine = 1.0 + x2 * (-0.5 + x2 * (1.0 / 24 + x2 * (-1.0 / 720 + x2 * (1.0 / 40320))))
        quarter = turn.astype(jnp.int32)
        odd = (quarter & 1) == 1
        sign = (1 - (quarter & 2)).astype(F32)
        sin_p = jnp.where(odd, cosine, sine) * sign
        cos_p = jnp.where(odd, -sine, cosine) * sign
        radial = sin_p * inv_q
        kind_c = tall(centre[3:4], 8)
        kind_n = tall(other[3:4], 8)
        kinds = row.astype(F32)
        features = jnp.concatenate(
            [radial, (kind_c == kinds).astype(F32), (kind_n == kinds).astype(F32), jnp.zeros(shape, F32)], axis=0
        ).astype(BF16)

        def active(half):
            t = jnp.tanh(half)
            p = 1.0 + t
            a = half * p
            return a.astype(BF16), p + a * (1.0 - t)

        act_0, slope_0 = active(dot(w_in, features))
        act_1, slope_1 = active(dot(half_mid[0], act_0))
        act_2, slope_2 = active(dot(half_mid[1], act_1))
        energy = dot(out_rows, act_2)
        cot_1 = (dot(back_1, slope_2.astype(BF16)) * slope_1).astype(BF16)
        cot_0 = (dot(back_0, cot_1) * slope_0).astype(BF16)
        grad = dot(back_in_w, cot_0)
        pull = grad * ((jnp.pi / 2) * freq * cos_p - radial) * inv_q
        pull = tall(jnp.sum(pull, axis=0, keepdims=True), 8) * inv_q
        live = (start + iota(shape, 1) < live_edges).astype(F32)
        values = jnp.where(row & 3 == 3, energy, delta * pull) * live
        values16 = doubled(split_rows(values)).astype(BF16)
        high_c16 = doubled(high_c.astype(F32)).astype(BF16)
        high_n16 = doubled(high_n.astype(F32)).astype(BF16)
        sum_c[...] += dot_nt(masked_rows(high_c16, values16, OWN_HI), hot_c[:, cols])
        sum_n[...] += dot_nt(masked_rows(high_n16, values16, ALL_HI), hot_n[:, cols])
        return carry

    sum_c[...] = jnp.zeros(sum_c.shape, F32)
    sum_n[...] = jnp.zeros(sum_n.shape, F32)
    lax.fori_loop(0, EDGES // CHUNK, edge_chunk, 0)

    def parts(k, c):
        at = 8 * (OWN_HI + GHOST_HI * k + c)
        return -join_rows(sum_n[at : at + 8, :])[0:4]

    backs = [remote(back.at[k], back_in.at[k], 8 + k, *OFFSETS[k]) for k in range(8)]
    for k in FAR + NEAR:
        for c in range(GHOST_HI):
            back[k, :, LO * c : LO * (c + 1)] = parts(k, c)
        backs[k].start()

    own = []
    for h in range(OWN_HI):
        at = 8 * h
        centred = join_rows(sum_c[at : at + 8, :])
        energy_out[0, :, LO * h : LO * (h + 1)] = centred[3:4]
        own.append(centred - join_rows(sum_n[at : at + 8, :]))

    returned = jnp.zeros((4, GHOSTS), F32)
    for k in NEAR + FAR:
        backs[k].wait_recv()
        returned = returned + back_in[k]
    values16 = doubled(split_rows(doubled(returned))).astype(BF16)
    high16 = doubled(lent_high.astype(F32)).astype(BF16)
    added = dot_nt(masked_rows(high16, values16, OWN_HI), hot_g[...])

    for h in range(OWN_HI):
        span = slice(LO * h, LO * (h + 1))
        force = (own[h] + join_rows(added[8 * h : 8 * h + 8]))[0:3]
        for r in range(3):
            force_out[0, r, :, span] = force[r : r + 1]
        speed = speeds[0:3, span] + force * step_ref[0:3, span]
        state[0:3, span] = pay[0:3, span] + TIME_STEP * speed
        state[3:6, span] = speed
    table = []
    for h in range(OWN_HI):
        value = state[:, LO * h : LO * (h + 1)]
        head = value.astype(BF16)
        table += [value, value - head.astype(F32)]
    product = dot(jnp.concatenate(table, axis=0).astype(BF16), hot_m[...])
    chosen = pick_rows(product, tall(mig_high, 16), 0, jnp.zeros((16, 8 * MIG), F32), 16)
    empty = jnp.where(iota((8, 1), 0) == 6, -1.0, 0.0)
    leaving = jnp.where(tall(mig_valid, 8) > 0.0, chosen[0:8] + chosen[8:16] + mig_shift, empty)
    for pair in range(4):
        mig_out[pair] = leaving[:, 2 * MIG * pair : 2 * MIG * (pair + 1)]
    moves = [remote(mig_out.at[k // 2], mig_in.at[k], 16 + k, *OFFSETS[k]) for k in range(8)]
    for copy in moves:
        copy.start()
    kept = jnp.where(gone[...] > 0.0, empty, state[...])
    for r in range(7):
        state_out[0, r, :, 0:ATOMS] = kept[r : r + 1]
    for copy in moves:
        copy.wait_recv()
    for pair in range(4):
        arrived = jnp.where(iota((8, 2 * MIG), 1) < MIG, mig_in[2 * pair], mig_in[2 * pair + 1])
        for r in range(7):
            state_out[0, r, :, ATOMS + 2 * MIG * pair : ATOMS + 2 * MIG * (pair + 1)] = arrived[r : r + 1]
    for copy in lends + backs + moves:
        copy.wait_send()


def shards(
    positions, velocities, species, masses, centers, neighbours, edge_count, ghost_list, mig_list, mig_count,
    w_rbf, embed_center, embed_neighbour, w_mid, w_out,
):
    vmem = pl.BlockSpec(memory_space=pltpu.VMEM)
    hbm = pl.BlockSpec(memory_space=pltpu.HBM)
    rows_first = functools.partial(jnp.transpose, axes=(0, 2, 1, 3))
    arguments = (
        rows_first(positions), rows_first(velocities), species, masses, centers, neighbours, edge_count.reshape(1, 1, 1), ghost_list,
        mig_list, mig_count, w_rbf.T, embed_center.T, embed_neighbour.T, w_mid, w_out.reshape(1, -1),
    )
    scalars = (3, 6, 9)
    local = [
        (pltpu.SMEM if n in scalars else pltpu.VMEM)(value.shape, value.dtype) for n, value in enumerate(arguments)
    ]
    energy, forces, new_state = pl.pallas_call(
        functools.partial(kernel, lax.axis_size("gx"), lax.axis_size("gy")),
        out_shape=(
            jax.ShapeDtypeStruct((1, 1, ATOMS), F32),
            jax.ShapeDtypeStruct((1, 3, 1, ATOMS), F32),
            jax.ShapeDtypeStruct((1, 7, 1, ATOMS + 8 * MIG), F32),
        ),
        in_specs=[hbm] * 15,
        out_specs=(vmem, vmem, vmem),
        scratch_shapes=local
        + [
            pltpu.VMEM((LO, max(CHUNK, GHOSTS)), BF16),
            pltpu.VMEM((8, ATOMS), F32),
            pltpu.VMEM((8 * OWN_HI, LO), BF16),
            pltpu.VMEM((32 * GHOST_HI, LO), BF16),
            pltpu.VMEM((32 * GHOST_HI, LO), BF16),
            pltpu.VMEM((LO, EDGES), BF16),
            pltpu.VMEM((LO, EDGES), BF16),
            pltpu.VMEM((LO, GHOSTS), BF16),
            pltpu.VMEM((LO, 8 * MIG), BF16),
            pltpu.VMEM((8, EDGES), jnp.int32),
            pltpu.VMEM((8, EDGES), jnp.int32),
            pltpu.VMEM((8, EDGES), F32),
            pltpu.VMEM((8, EDGES), F32),
            pltpu.VMEM((4, GHOSTS), F32),
            pltpu.VMEM((8, 4, GHOSTS), F32),
            pltpu.VMEM((8, 4, GHOSTS), F32),
            pltpu.VMEM((8, 4, GHOSTS), F32),
            pltpu.VMEM((8, ATOMS), F32),
            pltpu.VMEM((8, ATOMS), F32),
            pltpu.VMEM((8, ATOMS), F32),
            pltpu.VMEM((8, ATOMS), F32),
            pltpu.VMEM((8, 2 * MIG), jnp.int32),
            pltpu.VMEM((4, 8, 2 * MIG), F32),
            pltpu.VMEM((8, 8, 2 * MIG), F32),
            pltpu.VMEM((8 * OWN_HI, LO), F32),
            pltpu.VMEM((8 * ALL_HI, LO), F32),
            pltpu.SemaphoreType.DMA((24,)),
            pltpu.SemaphoreType.DMA((24,)),
            pltpu.SemaphoreType.DMA((15,)),
        ],
        compiler_params=pltpu.CompilerParams(
            collective_id=0, has_side_effects=True, vmem_limit_bytes=60 * 1024 * 1024
        ),
    )(*arguments)
    return (energy, rows_first(forces), rows_first(new_state))


def solution(mesh):
    return jax.shard_map(
        shards,
        mesh=mesh,
        in_specs=(
            P("gx", "gy", None, None),
            P("gx", "gy", None, None),
            P("gx", "gy", None),
            P(),
            P("gx", "gy", None),
            P("gx", "gy", None),
            P("gx", "gy"),
            P("gx", "gy", None),
            P("gx", "gy", None, None),
            P("gx", "gy", None),
            P(),
            P(),
            P(),
            P(),
            P(),
        ),
        out_specs=(P("gx", "gy", None), P("gx", "gy", None, None), P("gx", "gy", None, None)),
        check_vma=False,
    )
```

```python
import functools

import jax
import jax.numpy as jnp
from jax import lax
from jax.experimental import pallas as pl
from jax.experimental.pallas import tpu as pltpu
from jax.sharding import PartitionSpec as P

BOX_SIDE = 6.0
TIME_STEP = 0.1
NEAR = (1, 6, 3, 4)
FAR = (0, 2, 5, 7)
OFFSETS = ((-1, -1), (-1, 0), (-1, 1), (0, -1), (0, 1), (1, -1), (1, 0), (1, 1))

ATOMS = 2048
GHOSTS = 1024
EDGES = 4096
MIG = 64
LO = 256
OWN_HI = ATOMS // LO
GHOST_HI = GHOSTS // LO
ALL_HI = OWN_HI + 8 * GHOST_HI
CHUNK = 4096
MESH = pl.DeviceIdType.MESH
F32 = jnp.float32
BF16 = jnp.bfloat16


def dot(a, b):
    return jnp.dot(a, b, preferred_element_type=F32)


def dot_nt(a, b):
    return lax.dot_general(a, b, (((1,), (1,)), ((), ())), preferred_element_type=F32)


def iota(shape, dim):
    return lax.broadcasted_iota(jnp.int32, shape, dim)


def tall(row, height):
    return jnp.broadcast_to(row, (height, row.shape[1]))


def split_rows(both):
    head = both.astype(BF16).astype(F32)
    return jnp.where(iota(both.shape, 0) < 4, head, both - head)


def join_rows(both):
    return both + pltpu.roll(both, 4, 0)


def write_onehot(ref, cols, low, rows):
    low16 = tall(low, 16).astype(F32).astype(BF16)
    one = jnp.ones(low16.shape, BF16)
    zero = jnp.zeros(low16.shape, BF16)
    for i in range(LO // 16):
        span = pl.ds(16 * i, 16)
        ref[span, cols] = jnp.where(rows[span, 0 : low.shape[1]] == low16, one, zero)


def masked_rows(high16, values16, starts):
    step = (iota(values16.shape, 0) // 4).astype(F32)
    zero = jnp.zeros(values16.shape, BF16)
    return jnp.concatenate(
        [jnp.where(high16 == (step + float(start)).astype(BF16), values16, zero) for start in starts], axis=0
    )


def sixteen(eight_rows):
    return jnp.concatenate([eight_rows, eight_rows], axis=0).astype(BF16)


def table_of(rows):
    return jnp.concatenate(
        [rows[:, LO * h : LO * (h + 1)] for h in range(rows.shape[1] // LO)], axis=0
    ).astype(BF16)


def pick_rows(product, high, first, total, height=8):
    for h in range(product.shape[0] // height):
        total = jnp.where(high == first + h, product[height * h : height * (h + 1)], total)
    return total


def doubled(value):
    return jnp.concatenate([value, value], axis=0)


def kernel(
    nx, ny,
    *refs,
):
    inputs, outputs, local, refs = refs[:15], refs[15:18], refs[18:33], refs[33:]
    energy_out, force_out, state_out = outputs
    (
    rows_ref, pay, tab_own, tab_near, tab_far, hot_c, hot_n, hot_g, hot_m, hot_l, sel_c, sel_n,
    acc_c, acc_n, lend, ghosts, back, back_in, step_ref, speeds, state, gone, lists, mig_out, mig_in, own,
    send_sem, recv_sem, load_sem,
    ) = refs
    pos, vel, spec, mass, cen, nei, count, ghost, mig_list, mig_count, w_rbf, emb_c, emb_n, w_mid, w_out = local
    i = lax.axis_index("gx")
    j = lax.axis_index("gy")

    def device(first, second):
        return (lax.rem(i + first + nx, nx), lax.rem(j + second + ny, ny))

    def remote(src, dst, sem, first, second):
        return pltpu.make_async_remote_copy(
            src_ref=src, dst_ref=dst, send_sem=send_sem.at[sem], recv_sem=recv_sem.at[sem],
            device_id=device(first, second), device_id_type=MESH,
        )

    barrier = pltpu.get_barrier_semaphore()
    for first, second in OFFSETS:
        pl.semaphore_signal(barrier, inc=1, device_id=device(first, second), device_id_type=MESH)

    loads = [pltpu.make_async_copy(inputs[n], local[n], load_sem.at[n]) for n in range(15)]
    first_loads, later_loads = (0, 2, 7), (4, 5, 1, 3, 6, 8, 9, 10, 11, 12, 13, 14)
    for n in first_loads + later_loads:
        loads[n].start()

    rows_ref[...] = iota(rows_ref.shape, 0).astype(F32).astype(BF16)
    for n in first_loads:
        loads[n].wait()
    spec_row = spec[0].astype(F32)
    for r in range(3):
        pay[r : r + 1, :] = pos[0, r]
        pay[r + 4 : r + 5, :] = pos[0, r]
    pay[3:4, :] = spec_row
    pay[7:8, :] = spec_row
    tab_own[...] = table_of(split_rows(pay[...]))
    lent = ghost[0]
    write_onehot(hot_g, pl.ds(0, GHOSTS), lent & (LO - 1), rows_ref)
    lent_high = tall(lent // LO, 8)
    picked = pick_rows(dot(tab_own[...], hot_g[...]), lent_high, 0, jnp.zeros((8, GHOSTS), F32))
    lend[...] = join_rows(picked)[0:4]

    pl.semaphore_wait(barrier, 8)

    lends = [remote(lend, ghosts.at[k], k, *OFFSETS[7 - k]) for k in range(8)]
    for k in FAR + NEAR:
        lends[k].start()
    for n in later_loads:
        loads[n].wait()

    def own_chunk(step):
        cols = pl.ds(step * CHUNK, CHUNK)
        for index, hot, sel, acc in ((cen, hot_c, sel_c, acc_c), (nei, hot_n, sel_n, acc_n)):
            place = index[0, :, cols]
            write_onehot(hot, cols, place & (LO - 1), rows_ref)
            high = tall(place // LO, 8)
            sel[:, cols] = high
            acc[:, cols] = pick_rows(dot(tab_own[...], hot[:, cols]), high, 0, jnp.zeros((8, CHUNK), F32))

    own_chunk(0)

    inverse = jnp.zeros((1, ATOMS), F32)
    for kind in range(5):
        inverse = jnp.where(spec_row == float(kind), 1.0 / jnp.full((1, ATOMS), mass[kind], F32), inverse)
    step_row = TIME_STEP * inverse
    step_ref[...] = tall(step_row, 8)
    for r in range(3):
        speeds[r : r + 1, :] = vel[0, r]
        speeds[r + 4 : r + 5, :] = vel[0, r]
    speeds[3:4, :] = step_row
    speeds[7:8, :] = step_row
    state[...] = jnp.zeros(state.shape, F32)
    state[6:7, :] = spec_row
    lists[...] = jnp.zeros(lists.shape, jnp.int32)
    lists[:, 0:MIG] = mig_list[0, 0]
    listed = lists[...]
    moved = pltpu.roll(listed, MIG, 1)
    lane = iota((1, 2 * MIG), 1)
    mig_place = []
    mig_high = []
    mig_shift = []
    mig_valid = []
    for pair in range(4):
        place = jnp.where(lane < MIG, listed[2 * pair : 2 * pair + 1], moved[2 * pair + 1 : 2 * pair + 2])
        write_onehot(hot_m, pl.ds(2 * MIG * pair, 2 * MIG), place & (LO - 1), rows_ref)
        mig_place.append(place)
        mig_high.append(place // LO)
        limit = jnp.where(lane < MIG, mig_count[0, 0, 2 * pair], mig_count[0, 0, 2 * pair + 1] + MIG)
        mig_valid.append((lane < limit).astype(F32))
        row = iota((8, 2 * MIG), 0)
        half = iota((8, 2 * MIG), 1) < MIG
        (a0, b0), (a1, b1) = OFFSETS[2 * pair], OFFSETS[2 * pair + 1]
        mig_shift.append(
            jnp.where(row == 0, jnp.where(half, -BOX_SIDE * a0, -BOX_SIDE * a1), 0.0)
            + jnp.where(row == 1, jnp.where(half, -BOX_SIDE * b0, -BOX_SIDE * b1), 0.0)
        )
    mig_place = jnp.concatenate(mig_place, axis=1)
    mig_high = jnp.concatenate(mig_high, axis=1)
    mig_shift = jnp.concatenate(mig_shift, axis=1)
    mig_valid = jnp.concatenate(mig_valid, axis=1)
    leaving = masked_rows(
        tall(mig_high, 16).astype(F32).astype(BF16), tall(mig_valid, 16).astype(BF16), (0, 4)
    )
    left = dot_nt(leaving, hot_m[...])
    for h in range(OWN_HI):
        gone[:, LO * h : LO * (h + 1)] = tall(left[4 * h : 4 * h + 1], 8)

    mig_high8 = tall(mig_high, 8)

    def leave(table):
        return join_rows(pick_rows(dot(table, hot_m[...]), mig_high8, 0, jnp.zeros((8, 8 * MIG), F32)))

    mig_pos = leave(tab_own[...])
    mig_speed = leave(table_of(split_rows(speeds[...])))
    mig_step = tall(mig_speed[3:4], 8)
    mig_kind = tall(mig_pos[3:4], 8)
    lent_column = tall(lent.astype(F32), 8).T[:, 0:1]
    hot_l[...] = (lent_column == mig_place.astype(F32)).astype(F32).astype(BF16)

    def eight(weights):
        values = weights.astype(F32)
        short = 8 - values.shape[0]
        return jnp.concatenate([values, jnp.zeros((short, values.shape[1]), F32)], axis=0) if short else values

    rbf = 0.5 * w_rbf[...].astype(F32)
    w_in = jnp.concatenate([rbf, 0.5 * eight(emb_c[...]), 0.5 * eight(emb_n[...]), jnp.zeros(rbf.shape, F32)], axis=0).T.astype(BF16)
    mid = [w_mid[layer].astype(F32) for layer in range(2)]
    half_mid = [(0.5 * w).astype(BF16) for w in mid]
    out_row = w_out[...].astype(F32)
    out_rows = tall(out_row, 8).astype(BF16)
    back_1 = (0.5 * mid[1].T * out_row).astype(BF16)
    back_0 = (0.5 * mid[0].T).astype(BF16)
    back_in_w = rbf.astype(BF16)

    def ghost_table(ref, blocks):
        for m, k in enumerate(blocks):
            lends[k].wait_recv()
            size = 8 * GHOST_HI
            ref[size * m : size * (m + 1), :] = table_of(split_rows(doubled(ghosts[k])))

    def pick_ghosts(ref, blocks, cols, total):
        product = dot(ref[...], hot_n[:, cols])
        high = sel_n[:, cols]
        size = 8 * GHOST_HI
        for m, k in enumerate(blocks):
            total = pick_rows(product[size * m : size * (m + 1)], high, OWN_HI + GHOST_HI * k, total)
        return total

    def near_chunk(step):
        cols = pl.ds(step * CHUNK, CHUNK)
        acc_n[:, cols] = pick_ghosts(tab_near, NEAR, cols, acc_n[:, cols])

    ghost_table(tab_near, NEAR)
    near_chunk(0)
    ghost_table(tab_far, FAR)

    live_edges = count[0, 0, 0]

    def edge_chunk(step):
        start = step * CHUNK
        cols = pl.ds(start, CHUNK)
        shape = (8, CHUNK)
        row = iota(shape, 0)
        high_n = sel_n[:, cols]
        high_c = sel_c[:, cols]
        other = pick_ghosts(tab_far, FAR, cols, acc_n[:, cols])
        other = join_rows(other)
        centre = join_rows(acc_c[:, cols])
        block = (high_n - OWN_HI) // GHOST_HI
        cell = block + (block >= 4).astype(jnp.int32)
        third = (cell * 11) >> 5
        side = jnp.where(row & 3 == 0, third - 1, jnp.where(row & 3 == 1, cell - 3 * third - 1, 0))
        side = jnp.where(high_n < OWN_HI, 0, side)
        delta = other - centre + BOX_SIDE * side.astype(F32)
        square = jnp.sum(jnp.where(row < 3, delta * delta, 0.0), axis=0, keepdims=True) + 1.0
        q = tall(jnp.sqrt(square), 8)
        inv_q = 1.0 / q
        freq = (row + 1).astype(F32)
        phase = freq * q
        turn = jnp.floor(phase + 0.5)
        x = (phase - turn) * (jnp.pi / 2)
        x2 = x * x
        sine = x * (1.0 + x2 * (-1.0 / 6 + x2 * (1.0 / 120 + x2 * (-1.0 / 5040 + x2 * (1.0 / 362880)))))
        cosine = 1.0 + x2 * (-0.5 + x2 * (1.0 / 24 + x2 * (-1.0 / 720 + x2 * (1.0 / 40320))))
        quarter = turn.astype(jnp.int32)
        odd = (quarter & 1) == 1
        sign = (1 - (quarter & 2)).astype(F32)
        sin_p = jnp.where(odd, cosine, sine) * sign
        cos_p = jnp.where(odd, -sine, cosine) * sign
        radial = sin_p * inv_q
        kind_c = tall(centre[3:4], 8)
        kind_n = tall(other[3:4], 8)
        kinds = row.astype(F32)
        features = jnp.concatenate(
            [radial, (kind_c == kinds).astype(F32), (kind_n == kinds).astype(F32), jnp.zeros(shape, F32)], axis=0
        ).astype(BF16)

        def active(half):
            t = jnp.tanh(half)
            p = 1.0 + t
            a = half * p
            return a.astype(BF16), p + a * (1.0 - t)

        act_0, slope_0 = active(dot(w_in, features))
        act_1, slope_1 = active(dot(half_mid[0], act_0))
        act_2, slope_2 = active(dot(half_mid[1], act_1))
        energy = dot(out_rows, act_2)
        cot_1 = (dot(back_1, slope_2.astype(BF16)) * slope_1).astype(BF16)
        cot_0 = (dot(back_0, cot_1) * slope_0).astype(BF16)
        grad = dot(back_in_w, cot_0)
        pull = grad * ((jnp.pi / 2) * freq * cos_p - radial) * inv_q
        pull = tall(jnp.sum(pull, axis=0, keepdims=True), 8) * inv_q
        live = (start + iota(shape, 1) < live_edges).astype(F32)
        values = jnp.where(row & 3 == 3, energy, delta * pull) * live
        return sixteen(values), sixteen(high_c.astype(F32)), sixteen(high_n.astype(F32))

    values16, high_c16, high_n16 = edge_chunk(0)

    backs = [remote(back.at[k], back_in.at[k], 8 + k, *OFFSETS[k]) for k in range(8)]
    order = FAR + NEAR
    ghost_sum = dot_nt(masked_rows(high_n16, values16, [OWN_HI + GHOST_HI * k for k in order]), hot_n[...])
    for m, k in enumerate(order):
        for c in range(GHOST_HI):
            at = 4 * (GHOST_HI * m + c)
            back[k, :, LO * c : LO * (c + 1)] = -ghost_sum[at : at + 4]
        backs[k].start()

    sum_c = dot_nt(masked_rows(high_c16, values16, (0, 4)), hot_c[...])
    sum_n = dot_nt(masked_rows(high_n16, values16, (0, 4)), hot_n[...])
    own_sum = sum_c - sum_n
    for h in range(OWN_HI):
        span = slice(LO * h, LO * (h + 1))
        energy_out[0, :, span] = sum_c[4 * h + 3 : 4 * h + 4]
        own[0:4, span] = own_sum[4 * h : 4 * h + 4]
        own[4:8, span] = own_sum[4 * h : 4 * h + 4]
    mig_force = leave(table_of(split_rows(own[...])))

    returned = jnp.zeros((4, GHOSTS), F32)
    for k in NEAR + FAR:
        backs[k].wait_recv()
        returned = returned + back_in[k]
    halves = split_rows(doubled(returned))

    row = iota((8, 8 * MIG), 0)
    mig_force = mig_force + join_rows(dot(sixteen(halves), hot_l[...])[0:8])
    mig_speed = mig_speed + mig_force * mig_step
    mig_pos = mig_pos + TIME_STEP * mig_speed
    carried = jnp.where(row < 3, mig_pos, jnp.where(row < 6, pltpu.roll(mig_speed, 3, 0), mig_kind))
    empty = jnp.where(iota((8, 1), 0) == 6, -1.0, 0.0)
    carried = jnp.where(tall(mig_valid, 8) > 0.0, carried + mig_shift, empty)
    for pair in range(4):
        mig_out[pair] = carried[:, 2 * MIG * pair : 2 * MIG * (pair + 1)]
    moves = [remote(mig_out.at[k // 2], mig_in.at[k], 16 + k, *OFFSETS[k]) for k in range(8)]
    for k in FAR + NEAR:
        moves[k].start()

    lent_high16 = sixteen(lent_high.astype(F32))
    added = dot_nt(
        jnp.concatenate(
            [masked_rows(lent_high16, sixteen(doubled(part)), (0, 4)) for part in (halves[0:4], halves[4:8])], axis=0
        ),
        hot_g[...],
    )
    added = added[0 : 4 * OWN_HI] + added[4 * OWN_HI :]
    for h in range(OWN_HI):
        span = slice(LO * h, LO * (h + 1))
        force = own[0:3, span] + added[4 * h : 4 * h + 3]
        for r in range(3):
            force_out[0, r, :, span] = force[r : r + 1]
        speed = speeds[0:3, span] + force * step_ref[0:3, span]
        state[0:3, span] = pay[0:3, span] + TIME_STEP * speed
        state[3:6, span] = speed
    kept = jnp.where(gone[...] > 0.0, empty, state[...])
    for r in range(7):
        state_out[0, r, :, 0:ATOMS] = kept[r : r + 1]
    for copy in moves:
        copy.wait_recv()
    for pair in range(4):
        arrived = jnp.where(iota((8, 2 * MIG), 1) < MIG, mig_in[2 * pair], mig_in[2 * pair + 1])
        for r in range(7):
            state_out[0, r, :, ATOMS + 2 * MIG * pair : ATOMS + 2 * MIG * (pair + 1)] = arrived[r : r + 1]
    for copy in lends + backs + moves:
        copy.wait_send()


def hand_over(energy, forces, new_state, energy_out, force_out, state_out, sem):
    copies = [
        pltpu.make_async_copy(source, target, sem.at[n])
        for n, (source, target) in enumerate(((energy, energy_out), (forces, force_out), (new_state, state_out)))
    ]
    for copy in copies:
        copy.start()
    for copy in copies:
        copy.wait()


def shards(
    positions, velocities, species, masses, centers, neighbours, edge_count, ghost_list, mig_list, mig_count,
    w_rbf, embed_center, embed_neighbour, w_mid, w_out,
):
    vmem = pl.BlockSpec(memory_space=pltpu.VMEM)
    hbm = pl.BlockSpec(memory_space=pltpu.HBM)
    rows_first = functools.partial(jnp.transpose, axes=(0, 2, 1, 3))
    arguments = (
        rows_first(positions), rows_first(velocities), species, masses, centers, neighbours, edge_count.reshape(1, 1, 1), ghost_list,
        mig_list, mig_count, w_rbf.T, embed_center.T, embed_neighbour.T, w_mid, w_out.reshape(1, -1),
    )
    scalars = (3, 6, 9)
    local = [
        (pltpu.SMEM if n in scalars else pltpu.VMEM)(value.shape, value.dtype) for n, value in enumerate(arguments)
    ]
    energy, forces, new_state = pl.pallas_call(
        functools.partial(kernel, lax.axis_size("gx"), lax.axis_size("gy")),
        out_shape=(
            pltpu.VMEM((1, 1, ATOMS), F32),
            pltpu.VMEM((1, 3, 1, ATOMS), F32),
            pltpu.VMEM((1, 7, 1, ATOMS + 8 * MIG), F32),
        ),
        in_specs=[hbm] * 15,
        out_specs=(vmem, vmem, vmem),
        scratch_shapes=local
        + [
            pltpu.VMEM((LO, max(CHUNK, GHOSTS)), BF16),
            pltpu.VMEM((8, ATOMS), F32),
            pltpu.VMEM((8 * OWN_HI, LO), BF16),
            pltpu.VMEM((32 * GHOST_HI, LO), BF16),
            pltpu.VMEM((32 * GHOST_HI, LO), BF16),
            pltpu.VMEM((LO, EDGES), BF16),
            pltpu.VMEM((LO, EDGES), BF16),
            pltpu.VMEM((LO, GHOSTS), BF16),
            pltpu.VMEM((LO, 8 * MIG), BF16),
            pltpu.VMEM((GHOSTS, 8 * MIG), BF16),
            pltpu.VMEM((8, EDGES), jnp.int32),
            pltpu.VMEM((8, EDGES), jnp.int32),
            pltpu.VMEM((8, EDGES), F32),
            pltpu.VMEM((8, EDGES), F32),
            pltpu.VMEM((4, GHOSTS), F32),
            pltpu.VMEM((8, 4, GHOSTS), F32),
            pltpu.VMEM((8, 4, GHOSTS), F32),
            pltpu.VMEM((8, 4, GHOSTS), F32),
            pltpu.VMEM((8, ATOMS), F32),
            pltpu.VMEM((8, ATOMS), F32),
            pltpu.VMEM((8, ATOMS), F32),
            pltpu.VMEM((8, ATOMS), F32),
            pltpu.VMEM((8, 2 * MIG), jnp.int32),
            pltpu.VMEM((4, 8, 2 * MIG), F32),
            pltpu.VMEM((8, 8, 2 * MIG), F32),
            pltpu.VMEM((8, ATOMS), F32),
            pltpu.SemaphoreType.DMA((24,)),
            pltpu.SemaphoreType.DMA((24,)),
            pltpu.SemaphoreType.DMA((15,)),
        ],
        compiler_params=pltpu.CompilerParams(
            collective_id=0, has_side_effects=True, vmem_limit_bytes=60 * 1024 * 1024
        ),
    )(*arguments)
    results = pl.pallas_call(
        hand_over,
        out_shape=tuple(jax.ShapeDtypeStruct(value.shape, F32) for value in (energy, forces, new_state)),
        in_specs=[vmem] * 3,
        out_specs=(hbm, hbm, hbm),
        scratch_shapes=[pltpu.SemaphoreType.DMA((3,))],
    )(*(pltpu.with_memory_space_constraint(value, pltpu.VMEM) for value in (energy, forces, new_state)))
    return (results[0], rows_first(results[1]), rows_first(results[2]))


def solution(mesh):
    return jax.shard_map(
        shards,
        mesh=mesh,
        in_specs=(
            P("gx", "gy", None, None),
            P("gx", "gy", None, None),
            P("gx", "gy", None),
            P(),
            P("gx", "gy", None),
            P("gx", "gy", None),
            P("gx", "gy"),
            P("gx", "gy", None),
            P("gx", "gy", None, None),
            P("gx", "gy", None),
            P(),
            P(),
            P(),
            P(),
            P(),
        ),
        out_specs=(P("gx", "gy", None), P("gx", "gy", None, None), P("gx", "gy", None, None)),
        check_vma=False,
    )
```

```python
import functools

import jax
import jax.numpy as jnp
from jax import lax
from jax.experimental import pallas as pl
from jax.experimental.pallas import tpu as pltpu
from jax.sharding import PartitionSpec as P

BOX_SIDE = 6.0
TIME_STEP = 0.1
NEAR = (1, 6, 3, 4)
FAR = (0, 2, 5, 7)
OFFSETS = ((-1, -1), (-1, 0), (-1, 1), (0, -1), (0, 1), (1, -1), (1, 0), (1, 1))

ATOMS = 2048
GHOSTS = 1024
EDGES = 4096
MIG = 64
LO = 256
OWN_HI = ATOMS // LO
GHOST_HI = GHOSTS // LO
ALL_HI = OWN_HI + 8 * GHOST_HI
CHUNK = 4096
MESH = pl.DeviceIdType.MESH
F32 = jnp.float32
BF16 = jnp.bfloat16


def dot(a, b):
    return jnp.dot(a, b, preferred_element_type=F32)


def dot_nt(a, b):
    return lax.dot_general(a, b, (((1,), (1,)), ((), ())), preferred_element_type=F32)


def iota(shape, dim):
    return lax.broadcasted_iota(jnp.int32, shape, dim)


def tall(row, height):
    return jnp.broadcast_to(row, (height, row.shape[1]))


def split_rows(both):
    head = both.astype(BF16).astype(F32)
    return jnp.where(iota(both.shape, 0) < 4, head, both - head)


def join_rows(both):
    return both + pltpu.roll(both, 4, 0)


def write_onehot(ref, cols, low, rows):
    low16 = tall(low, 16).astype(F32).astype(BF16)
    one = jnp.ones(low16.shape, BF16)
    zero = jnp.zeros(low16.shape, BF16)
    for i in range(LO // 16):
        span = pl.ds(16 * i, 16)
        ref[span, cols] = jnp.where(rows[span, 0 : low.shape[1]] == low16, one, zero)


def masked_rows(high16, values16, starts):
    step = (iota(values16.shape, 0) & 3).astype(F32)
    zero = jnp.zeros(values16.shape, BF16)
    return jnp.concatenate(
        [jnp.where(high16 == (step + float(start)).astype(BF16), values16, zero) for start in starts], axis=0
    )


def spread_rows(eight_rows):
    fours = [tall(eight_rows[r : r + 1], 8) for r in range(4)]
    upper = iota(eight_rows.shape, 0) >= 4
    return jnp.concatenate(
        [jnp.where(upper, fours[1], fours[0]), jnp.where(upper, fours[3], fours[2])], axis=0
    ).astype(BF16)


def sixteen(eight_rows):
    return jnp.concatenate([eight_rows, eight_rows], axis=0).astype(BF16)


def table_of(rows):
    return jnp.concatenate(
        [rows[:, LO * h : LO * (h + 1)] for h in range(rows.shape[1] // LO)], axis=0
    ).astype(BF16)


def pick_rows(product, high, first, total, height=8):
    for h in range(product.shape[0] // height):
        total = jnp.where(high == first + h, product[height * h : height * (h + 1)], total)
    return total


def doubled(value):
    return jnp.concatenate([value, value], axis=0)


def kernel(
    nx, ny,
    *refs,
):
    inputs, outputs, local, refs = refs[:15], refs[15:18], refs[18:33], refs[33:]
    energy_out, force_out, state_out = outputs
    (
    rows_ref, pay, tab_own, tab_near, tab_far, hot_c, hot_n, hot_g, hot_m, hot_l, sel_c, sel_n,
    acc_c, acc_n, lend, ghosts, back, back_in, total, step_ref, speeds, state, gone, lists, mig_out, mig_in, own,
    send_sem, recv_sem, load_sem,
    ) = refs
    pos, vel, spec, mass, cen, nei, count, ghost, mig_list, mig_count, w_rbf, emb_c, emb_n, w_mid, w_out = local
    i = lax.axis_index("gx")
    j = lax.axis_index("gy")

    def device(first, second):
        return (lax.rem(i + first + nx, nx), lax.rem(j + second + ny, ny))

    def remote(src, dst, sem, first, second):
        return pltpu.make_async_remote_copy(
            src_ref=src, dst_ref=dst, send_sem=send_sem.at[sem], recv_sem=recv_sem.at[sem],
            device_id=device(first, second), device_id_type=MESH,
        )

    barrier = pltpu.get_barrier_semaphore()
    for first, second in OFFSETS:
        pl.semaphore_signal(barrier, inc=1, device_id=device(first, second), device_id_type=MESH)

    loads = [pltpu.make_async_copy(inputs[n], local[n], load_sem.at[n]) for n in range(15)]
    first_loads, later_loads = (0, 2, 7), (4, 5, 1, 3, 6, 8, 9, 10, 11, 12, 13, 14)
    for n in first_loads + later_loads:
        loads[n].start()

    rows_ref[...] = iota(rows_ref.shape, 0).astype(F32).astype(BF16)
    for n in first_loads:
        loads[n].wait()
    spec_row = spec[0].astype(F32)
    for r in range(3):
        pay[r : r + 1, :] = pos[0, r]
        pay[r + 4 : r + 5, :] = pos[0, r]
    pay[3:4, :] = spec_row
    pay[7:8, :] = spec_row
    tab_own[...] = table_of(split_rows(pay[...]))
    lent = ghost[0]
    write_onehot(hot_g, pl.ds(0, GHOSTS), lent & (LO - 1), rows_ref)
    lent_high = tall(lent // LO, 8)
    picked = pick_rows(dot(tab_own[...], hot_g[...]), lent_high, 0, jnp.zeros((8, GHOSTS), F32))
    lend[...] = join_rows(picked)[0:4]

    pl.semaphore_wait(barrier, 8)

    lends = [remote(lend, ghosts.at[k], k, *OFFSETS[7 - k]) for k in range(8)]
    for k in FAR + (3, 4, 1, 6):
        lends[7 - k].start()
    for n in later_loads:
        loads[n].wait()

    def own_chunk(step):
        cols = pl.ds(step * CHUNK, CHUNK)
        for index, hot, sel, acc in ((cen, hot_c, sel_c, acc_c), (nei, hot_n, sel_n, acc_n)):
            place = index[0, :, cols]
            write_onehot(hot, cols, place & (LO - 1), rows_ref)
            high = tall(place // LO, 8)
            sel[:, cols] = high
            acc[:, cols] = pick_rows(dot(tab_own[...], hot[:, cols]), high, 0, jnp.zeros((8, CHUNK), F32))

    own_chunk(0)

    inverse = jnp.zeros((1, ATOMS), F32)
    for kind in range(5):
        inverse = jnp.where(spec_row == float(kind), 1.0 / jnp.full((1, ATOMS), mass[kind], F32), inverse)
    step_row = TIME_STEP * inverse
    step_ref[...] = tall(step_row, 8)
    for r in range(3):
        speeds[r : r + 1, :] = vel[0, r]
        speeds[r + 4 : r + 5, :] = vel[0, r]
    speeds[3:4, :] = step_row
    speeds[7:8, :] = step_row
    state[...] = jnp.zeros(state.shape, F32)
    state[6:7, :] = spec_row
    lists[...] = jnp.zeros(lists.shape, jnp.int32)
    lists[:, 0:MIG] = mig_list[0, 0]
    listed = lists[...]
    moved = pltpu.roll(listed, MIG, 1)
    lane = iota((1, 2 * MIG), 1)
    mig_place = []
    mig_high = []
    mig_shift = []
    mig_valid = []
    for pair in range(4):
        place = jnp.where(lane < MIG, listed[2 * pair : 2 * pair + 1], moved[2 * pair + 1 : 2 * pair + 2])
        write_onehot(hot_m, pl.ds(2 * MIG * pair, 2 * MIG), place & (LO - 1), rows_ref)
        mig_place.append(place)
        mig_high.append(place // LO)
        limit = jnp.where(lane < MIG, mig_count[0, 0, 2 * pair], mig_count[0, 0, 2 * pair + 1] + MIG)
        mig_valid.append((lane < limit).astype(F32))
        row = iota((8, 2 * MIG), 0)
        half = iota((8, 2 * MIG), 1) < MIG
        (a0, b0), (a1, b1) = OFFSETS[2 * pair], OFFSETS[2 * pair + 1]
        mig_shift.append(
            jnp.where(row == 0, jnp.where(half, -BOX_SIDE * a0, -BOX_SIDE * a1), 0.0)
            + jnp.where(row == 1, jnp.where(half, -BOX_SIDE * b0, -BOX_SIDE * b1), 0.0)
        )
    mig_place = jnp.concatenate(mig_place, axis=1)
    mig_high = jnp.concatenate(mig_high, axis=1)
    mig_shift = jnp.concatenate(mig_shift, axis=1)
    mig_valid = jnp.concatenate(mig_valid, axis=1)
    leaving = masked_rows(
        tall(mig_high, 16).astype(F32).astype(BF16), tall(mig_valid, 16).astype(BF16), (0, 4)
    )
    left = dot_nt(leaving, hot_m[...])
    for h in range(OWN_HI):
        at = 16 * (h // 4) + h % 4
        gone[:, LO * h : LO * (h + 1)] = tall(left[at : at + 1], 8)

    mig_high8 = tall(mig_high, 8)

    def leave(table):
        return join_rows(pick_rows(dot(table, hot_m[...]), mig_high8, 0, jnp.zeros((8, 8 * MIG), F32)))

    mig_pos = leave(tab_own[...])
    mig_speed = leave(table_of(split_rows(speeds[...])))
    mig_step = tall(mig_speed[3:4], 8)
    mig_kind = tall(mig_pos[3:4], 8)
    lent_column = tall(lent.astype(F32), 8).T[:, 0:1]
    hot_l[...] = (lent_column == mig_place.astype(F32)).astype(F32).astype(BF16)

    def eight(weights):
        values = weights.astype(F32)
        short = 8 - values.shape[0]
        return jnp.concatenate([values, jnp.zeros((short, values.shape[1]), F32)], axis=0) if short else values

    rbf = 0.5 * w_rbf[...].astype(F32)
    w_in = jnp.concatenate([rbf, 0.5 * eight(emb_c[...]), 0.5 * eight(emb_n[...]), jnp.zeros(rbf.shape, F32)], axis=0).T.astype(BF16)
    mid = [w_mid[layer].astype(F32) for layer in range(2)]
    half_mid = [(0.5 * w).astype(BF16) for w in mid]
    out_row = w_out[...].astype(F32)
    out_rows = tall(out_row, 8).astype(BF16)
    back_1 = (0.5 * mid[1].T * out_row).astype(BF16)
    back_0 = (0.5 * mid[0].T).astype(BF16)
    back_in_w = rbf.astype(BF16)

    def ghost_table(ref, blocks):
        for m, k in enumerate(blocks):
            lends[k].wait_recv()
            size = 8 * GHOST_HI
            ref[size * m : size * (m + 1), :] = table_of(split_rows(doubled(ghosts[k])))

    def pick_ghosts(ref, blocks, cols, total):
        product = dot(ref[...], hot_n[:, cols])
        high = sel_n[:, cols]
        size = 8 * GHOST_HI
        for m, k in enumerate(blocks):
            total = pick_rows(product[size * m : size * (m + 1)], high, OWN_HI + GHOST_HI * k, total)
        return total

    def near_chunk(step):
        cols = pl.ds(step * CHUNK, CHUNK)
        acc_n[:, cols] = pick_ghosts(tab_near, NEAR, cols, acc_n[:, cols])

    ghost_table(tab_near, NEAR)
    near_chunk(0)
    ghost_table(tab_far, FAR)

    live_edges = count[0, 0, 0]

    def edge_chunk(step):
        start = step * CHUNK
        cols = pl.ds(start, CHUNK)
        shape = (8, CHUNK)
        row = iota(shape, 0)
        high_n = sel_n[:, cols]
        high_c = sel_c[:, cols]
        other = pick_ghosts(tab_far, FAR, cols, acc_n[:, cols])
        other = join_rows(other)
        centre = join_rows(acc_c[:, cols])
        block = (high_n - OWN_HI) // GHOST_HI
        cell = block + (block >= 4).astype(jnp.int32)
        third = (cell * 11) >> 5
        side = jnp.where(row & 3 == 0, third - 1, jnp.where(row & 3 == 1, cell - 3 * third - 1, 0))
        side = jnp.where(high_n < OWN_HI, 0, side)
        delta = other - centre + BOX_SIDE * side.astype(F32)
        square = jnp.sum(jnp.where(row < 3, delta * delta, 0.0), axis=0, keepdims=True) + 1.0
        q = tall(jnp.sqrt(square), 8)
        inv_q = 1.0 / q
        freq = (row + 1).astype(F32)
        phase = freq * q
        turn = jnp.floor(phase + 0.5)
        x = (phase - turn) * (jnp.pi / 2)
        x2 = x * x
        sine = x * (1.0 + x2 * (-1.0 / 6 + x2 * (1.0 / 120 + x2 * (-1.0 / 5040 + x2 * (1.0 / 362880)))))
        cosine = 1.0 + x2 * (-0.5 + x2 * (1.0 / 24 + x2 * (-1.0 / 720 + x2 * (1.0 / 40320))))
        quarter = turn.astype(jnp.int32)
        odd = (quarter & 1) == 1
        sign = (1 - (quarter & 2)).astype(F32)
        sin_p = jnp.where(odd, cosine, sine) * sign
        cos_p = jnp.where(odd, -sine, cosine) * sign
        radial = sin_p * inv_q
        kind_c = tall(centre[3:4], 8)
        kind_n = tall(other[3:4], 8)
        kinds = row.astype(F32)
        features = jnp.concatenate(
            [radial, (kind_c == kinds).astype(F32), (kind_n == kinds).astype(F32), jnp.zeros(shape, F32)], axis=0
        ).astype(BF16)

        def active(half):
            t = jnp.tanh(half)
            p = 1.0 + t
            a = half * p
            return a.astype(BF16), p + a * (1.0 - t)

        act_0, slope_0 = active(dot(w_in, features))
        act_1, slope_1 = active(dot(half_mid[0], act_0))
        act_2, slope_2 = active(dot(half_mid[1], act_1))
        cot_1 = (dot(back_1, slope_2.astype(BF16)) * slope_1).astype(BF16)
        cot_0 = (dot(back_0, cot_1) * slope_0).astype(BF16)
        grad = dot(back_in_w, cot_0)
        pull = grad * ((jnp.pi / 2) * freq * cos_p - radial) * inv_q
        pull = tall(jnp.sum(pull, axis=0, keepdims=True), 8) * inv_q
        live = (start + iota(shape, 1) < live_edges).astype(F32)
        slopes = delta * pull * live
        return slopes, act_2, live, sixteen(high_c.astype(F32)), sixteen(high_n.astype(F32))

    slopes, act_2, live, high_c16, high_n16 = edge_chunk(0)

    backs = [remote(back.at[k], back_in.at[k], 8 + k, *OFFSETS[k]) for k in range(8)]
    slopes16 = spread_rows(-slopes)
    for blocks in (FAR, NEAR):
        ghost_sum = dot_nt(masked_rows(high_n16, slopes16, [OWN_HI + GHOST_HI * k for k in blocks]), hot_n[...])
        for m, k in enumerate(blocks):
            for r in range(3):
                back[k, r] = ghost_sum[16 * m + 4 * r : 16 * m + 4 * r + 4]
        for k in blocks:
            backs[k].start()

    energy = dot(out_rows, act_2) * live
    values16 = spread_rows(jnp.where(iota(slopes.shape, 0) == 3, energy, slopes))
    sum_c = dot_nt(masked_rows(high_c16, values16, (0, 4)), hot_c[...])
    own_sum = sum_c + dot_nt(masked_rows(high_n16, slopes16, (0, 4)), hot_n[...])
    for h in range(OWN_HI):
        span = slice(LO * h, LO * (h + 1))
        at = 16 * (h // 4) + h % 4
        energy_out[0, :, span] = sum_c[at + 12 : at + 13]
        for r in range(4):
            own[r : r + 1, span] = own_sum[at + 4 * r : at + 4 * r + 1]
            own[r + 4 : r + 5, span] = own_sum[at + 4 * r : at + 4 * r + 1]
    mig_force = leave(table_of(split_rows(own[...])))

    total[...] = jnp.zeros(total.shape, F32)
    returned = jnp.zeros((3, GHOST_HI, LO), F32)
    for k in NEAR + FAR:
        backs[k].wait_recv()
        returned = returned + back_in[k]
    for r in range(3):
        for c in range(GHOST_HI):
            span = slice(LO * c, LO * (c + 1))
            total[r : r + 1, span] = returned[r, c : c + 1]
            total[r + 4 : r + 5, span] = returned[r, c : c + 1]
    halves = split_rows(total[...])

    row = iota((8, 8 * MIG), 0)
    mig_force = mig_force + join_rows(dot(sixteen(halves), hot_l[...])[0:8])
    mig_speed = mig_speed + mig_force * mig_step
    mig_pos = mig_pos + TIME_STEP * mig_speed
    carried = jnp.where(row < 3, mig_pos, jnp.where(row < 6, pltpu.roll(mig_speed, 3, 0), mig_kind))
    empty = jnp.where(iota((8, 1), 0) == 6, -1.0, 0.0)
    carried = jnp.where(tall(mig_valid, 8) > 0.0, carried + mig_shift, empty)
    for pair in range(4):
        mig_out[pair] = carried[:, 2 * MIG * pair : 2 * MIG * (pair + 1)]
    moves = [remote(mig_out.at[k // 2], mig_in.at[k], 16 + k, *OFFSETS[k]) for k in range(8)]
    for k in FAR + (3, 4, 1, 6):
        moves[k].start()

    lent_high16 = sixteen(lent_high.astype(F32))
    added = dot_nt(
        jnp.concatenate(
            [masked_rows(lent_high16, spread_rows(doubled(part)), (0, 4)) for part in (halves[0:4], halves[4:8])], axis=0
        ),
        hot_g[...],
    )
    added = added[0 : 4 * OWN_HI] + added[4 * OWN_HI :]
    for h in range(OWN_HI):
        span = slice(LO * h, LO * (h + 1))
        at = 16 * (h // 4) + h % 4
        for r in range(3):
            force_row = own[r : r + 1, span] + added[at + 4 * r : at + 4 * r + 1]
            force_out[0, r, :, span] = force_row
            own[r : r + 1, span] = force_row
        force = own[0:3, span]
        speed = speeds[0:3, span] + force * step_ref[0:3, span]
        state[0:3, span] = pay[0:3, span] + TIME_STEP * speed
        state[3:6, span] = speed
    kept = jnp.where(gone[...] > 0.0, empty, state[...])
    for r in range(7):
        state_out[0, r, :, 0:ATOMS] = kept[r : r + 1]
    for copy in moves:
        copy.wait_recv()
    for pair in range(4):
        arrived = jnp.where(iota((8, 2 * MIG), 1) < MIG, mig_in[2 * pair], mig_in[2 * pair + 1])
        for r in range(7):
            state_out[0, r, :, ATOMS + 2 * MIG * pair : ATOMS + 2 * MIG * (pair + 1)] = arrived[r : r + 1]
    for copy in lends + backs + moves:
        copy.wait_send()


def hand_over(energy, forces, new_state, energy_out, force_out, state_out, sem):
    copies = [
        pltpu.make_async_copy(source, target, sem.at[n])
        for n, (source, target) in enumerate(((energy, energy_out), (forces, force_out), (new_state, state_out)))
    ]
    for copy in copies:
        copy.start()
    for copy in copies:
        copy.wait()


def shards(
    positions, velocities, species, masses, centers, neighbours, edge_count, ghost_list, mig_list, mig_count,
    w_rbf, embed_center, embed_neighbour, w_mid, w_out,
):
    vmem = pl.BlockSpec(memory_space=pltpu.VMEM)
    hbm = pl.BlockSpec(memory_space=pltpu.HBM)
    rows_first = functools.partial(jnp.transpose, axes=(0, 2, 1, 3))
    arguments = (
        rows_first(positions), rows_first(velocities), species, masses, centers, neighbours, edge_count.reshape(1, 1, 1), ghost_list,
        mig_list, mig_count, w_rbf.T, embed_center.T, embed_neighbour.T, w_mid, w_out.reshape(1, -1),
    )
    scalars = (3, 6, 9)
    local = [
        (pltpu.SMEM if n in scalars else pltpu.VMEM)(value.shape, value.dtype) for n, value in enumerate(arguments)
    ]
    energy, forces, new_state = pl.pallas_call(
        functools.partial(kernel, lax.axis_size("gx"), lax.axis_size("gy")),
        out_shape=(
            pltpu.VMEM((1, 1, ATOMS), F32),
            pltpu.VMEM((1, 3, 1, ATOMS), F32),
            pltpu.VMEM((1, 7, 1, ATOMS + 8 * MIG), F32),
        ),
        in_specs=[hbm] * 15,
        out_specs=(vmem, vmem, vmem),
        scratch_shapes=local
        + [
            pltpu.VMEM((LO, max(CHUNK, GHOSTS)), BF16),
            pltpu.VMEM((8, ATOMS), F32),
            pltpu.VMEM((8 * OWN_HI, LO), BF16),
            pltpu.VMEM((32 * GHOST_HI, LO), BF16),
            pltpu.VMEM((32 * GHOST_HI, LO), BF16),
            pltpu.VMEM((LO, EDGES), BF16),
            pltpu.VMEM((LO, EDGES), BF16),
            pltpu.VMEM((LO, GHOSTS), BF16),
            pltpu.VMEM((LO, 8 * MIG), BF16),
            pltpu.VMEM((GHOSTS, 8 * MIG), BF16),
            pltpu.VMEM((8, EDGES), jnp.int32),
            pltpu.VMEM((8, EDGES), jnp.int32),
            pltpu.VMEM((8, EDGES), F32),
            pltpu.VMEM((8, EDGES), F32),
            pltpu.VMEM((4, GHOSTS), F32),
            pltpu.VMEM((8, 4, GHOSTS), F32),
            pltpu.VMEM((8, 3, GHOST_HI, LO), F32),
            pltpu.VMEM((8, 3, GHOST_HI, LO), F32),
            pltpu.VMEM((8, GHOSTS), F32),
            pltpu.VMEM((8, ATOMS), F32),
            pltpu.VMEM((8, ATOMS), F32),
            pltpu.VMEM((8, ATOMS), F32),
            pltpu.VMEM((8, ATOMS), F32),
            pltpu.VMEM((8, 2 * MIG), jnp.int32),
            pltpu.VMEM((4, 8, 2 * MIG), F32),
            pltpu.VMEM((8, 8, 2 * MIG), F32),
            pltpu.VMEM((8, ATOMS), F32),
            pltpu.SemaphoreType.DMA((24,)),
            pltpu.SemaphoreType.DMA((24,)),
            pltpu.SemaphoreType.DMA((15,)),
        ],
        compiler_params=pltpu.CompilerParams(
            collective_id=0, has_side_effects=True, vmem_limit_bytes=60 * 1024 * 1024
        ),
    )(*arguments)
    results = pl.pallas_call(
        hand_over,
        out_shape=tuple(jax.ShapeDtypeStruct(value.shape, F32) for value in (energy, forces, new_state)),
        in_specs=[vmem] * 3,
        out_specs=(hbm, hbm, hbm),
        scratch_shapes=[pltpu.SemaphoreType.DMA((3,))],
    )(*(pltpu.with_memory_space_constraint(value, pltpu.VMEM) for value in (energy, forces, new_state)))
    return (results[0], rows_first(results[1]), rows_first(results[2]))


def solution(mesh):
    return jax.shard_map(
        shards,
        mesh=mesh,
        in_specs=(
            P("gx", "gy", None, None),
            P("gx", "gy", None, None),
            P("gx", "gy", None),
            P(),
            P("gx", "gy", None),
            P("gx", "gy", None),
            P("gx", "gy"),
            P("gx", "gy", None),
            P("gx", "gy", None, None),
            P("gx", "gy", None),
            P(),
            P(),
            P(),
            P(),
            P(),
        ),
        out_specs=(P("gx", "gy", None), P("gx", "gy", None, None), P("gx", "gy", None, None)),
        check_vma=False,
    )
```

```python
import functools

import jax
import jax.numpy as jnp
from jax import lax
from jax.experimental import pallas as pl
from jax.experimental.pallas import tpu as pltpu
from jax.sharding import PartitionSpec as P

BOX_SIDE = 6.0
TIME_STEP = 0.1
NEAR = (1, 6, 3, 4)
FAR = (0, 2, 5, 7)
OFFSETS = ((-1, -1), (-1, 0), (-1, 1), (0, -1), (0, 1), (1, -1), (1, 0), (1, 1))

ATOMS = 2048
GHOSTS = 1024
EDGES = 4096
MIG = 64
LO = 256
OWN_HI = ATOMS // LO
GHOST_HI = GHOSTS // LO
ALL_HI = OWN_HI + 8 * GHOST_HI
CHUNK = 4096
MESH = pl.DeviceIdType.MESH
F32 = jnp.float32
BF16 = jnp.bfloat16


def dot(a, b):
    return jnp.dot(a, b, preferred_element_type=F32)


def dot_nt(a, b):
    return lax.dot_general(a, b, (((1,), (1,)), ((), ())), preferred_element_type=F32)


def iota(shape, dim):
    return lax.broadcasted_iota(jnp.int32, shape, dim)


def tall(row, height):
    return jnp.broadcast_to(row, (height, row.shape[1]))


def split_rows(both):
    head = both.astype(BF16).astype(F32)
    return jnp.where(iota(both.shape, 0) < 4, head, both - head)


def join_rows(both):
    return both + pltpu.roll(both, 4, 0)


def write_onehot(ref, cols, low, rows):
    low16 = tall(low, 16).astype(F32).astype(BF16)
    one = jnp.ones(low16.shape, BF16)
    zero = jnp.zeros(low16.shape, BF16)
    for i in range(LO // 16):
        span = pl.ds(16 * i, 16)
        ref[span, cols] = jnp.where(rows[span, 0 : low.shape[1]] == low16, one, zero)


def masked_rows(high16, values16, starts):
    step = (iota(values16.shape, 0) & 3).astype(F32)
    zero = jnp.zeros(values16.shape, BF16)
    return jnp.concatenate(
        [jnp.where(high16 == (step + float(start)).astype(BF16), values16, zero) for start in starts], axis=0
    )


def spread_rows(eight_rows):
    fours = [tall(eight_rows[r : r + 1], 8) for r in range(4)]
    upper = iota(eight_rows.shape, 0) >= 4
    return jnp.concatenate(
        [jnp.where(upper, fours[1], fours[0]), jnp.where(upper, fours[3], fours[2])], axis=0
    ).astype(BF16)


def sixteen(eight_rows):
    return jnp.concatenate([eight_rows, eight_rows], axis=0).astype(BF16)


def table_of(rows):
    return jnp.concatenate(
        [rows[:, LO * h : LO * (h + 1)] for h in range(rows.shape[1] // LO)], axis=0
    ).astype(BF16)


def pick_rows(product, high, first, total, height=8):
    for h in range(product.shape[0] // height):
        total = jnp.where(high == first + h, product[height * h : height * (h + 1)], total)
    return total


def doubled(value):
    return jnp.concatenate([value, value], axis=0)


def kernel(
    nx, ny,
    *refs,
):
    inputs, outputs, local, refs = refs[:15], refs[15:18], refs[18:33], refs[33:]
    energy_out, force_out, state_out = outputs
    (
    rows_ref, pay, tab_own, tab_near, tab_far, hot_c, hot_n, hot_g, hot_m, hot_l, sel_c, sel_n,
    acc_c, acc_n, lend, ghosts, back, back_in, total, step_ref, speeds, state, gone, lists, mig_out, mig_in, own,
    send_sem, recv_sem, load_sem,
    ) = refs
    pos, vel, spec, mass, cen, nei, count, ghost, mig_list, mig_count, w_rbf, emb_c, emb_n, w_mid, w_out = local
    i = lax.axis_index("gx")
    j = lax.axis_index("gy")

    def device(first, second):
        return (lax.rem(i + first + nx, nx), lax.rem(j + second + ny, ny))

    def remote(src, dst, sem, first, second):
        return pltpu.make_async_remote_copy(
            src_ref=src, dst_ref=dst, send_sem=send_sem.at[sem], recv_sem=recv_sem.at[sem],
            device_id=device(first, second), device_id_type=MESH,
        )

    barrier = pltpu.get_barrier_semaphore()
    for first, second in OFFSETS:
        pl.semaphore_signal(barrier, inc=1, device_id=device(first, second), device_id_type=MESH)

    loads = [pltpu.make_async_copy(inputs[n], local[n], load_sem.at[n]) for n in range(15)]
    first_loads, later_loads = (0, 2, 7), (4, 5, 1, 3, 6, 8, 9, 10, 11, 12, 13, 14)
    for n in first_loads + later_loads:
        loads[n].start()

    rows_ref[...] = iota(rows_ref.shape, 0).astype(F32).astype(BF16)
    for n in first_loads:
        loads[n].wait()
    spec_row = spec[0].astype(F32)
    for r in range(3):
        pay[r : r + 1, :] = pos[0, r]
        pay[r + 4 : r + 5, :] = pos[0, r]
    pay[3:4, :] = spec_row
    pay[7:8, :] = spec_row
    tab_own[...] = table_of(split_rows(pay[...]))
    lent = ghost[0]
    write_onehot(hot_g, pl.ds(0, GHOSTS), lent & (LO - 1), rows_ref)
    lent_high = tall(lent // LO, 8)
    picked = pick_rows(dot(tab_own[...], hot_g[...]), lent_high, 0, jnp.zeros((8, GHOSTS), F32))
    lend[...] = join_rows(picked)[0:4]

    pl.semaphore_wait(barrier, 8)

    lends = [remote(lend, ghosts.at[k], k, *OFFSETS[7 - k]) for k in range(8)]
    for k in FAR + (3, 4, 1, 6):
        lends[7 - k].start()
    for n in later_loads:
        loads[n].wait()

    def own_chunk(step):
        cols = pl.ds(step * CHUNK, CHUNK)
        for index, hot, sel, acc in ((cen, hot_c, sel_c, acc_c), (nei, hot_n, sel_n, acc_n)):
            place = index[0, :, cols]
            write_onehot(hot, cols, place & (LO - 1), rows_ref)
            high = tall(place // LO, 8)
            sel[:, cols] = high
            acc[:, cols] = pick_rows(dot(tab_own[...], hot[:, cols]), high, 0, jnp.zeros((8, CHUNK), F32))

    own_chunk(0)

    def eight(weights):
        values = weights.astype(F32)
        short = 8 - values.shape[0]
        return jnp.concatenate([values, jnp.zeros((short, values.shape[1]), F32)], axis=0) if short else values

    rbf = 0.5 * w_rbf[...].astype(F32)
    w_in = jnp.concatenate([rbf, 0.5 * eight(emb_c[...]), 0.5 * eight(emb_n[...]), jnp.zeros(rbf.shape, F32)], axis=0).T.astype(BF16)
    mid = [w_mid[layer].astype(F32) for layer in range(2)]
    half_mid = [(0.5 * w).astype(BF16) for w in mid]
    out_row = w_out[...].astype(F32)
    out_rows = tall(out_row, 8).astype(BF16)
    back_1 = (0.5 * mid[1].T * out_row).astype(BF16)
    back_0 = (0.5 * mid[0].T).astype(BF16)
    back_in_w = rbf.astype(BF16)

    def ghost_table(ref, blocks):
        for m, k in enumerate(blocks):
            lends[k].wait_recv()
            size = 8 * GHOST_HI
            ref[size * m : size * (m + 1), :] = table_of(split_rows(doubled(ghosts[k])))

    def pick_ghosts(ref, blocks, cols, total):
        product = dot(ref[...], hot_n[:, cols])
        high = sel_n[:, cols]
        size = 8 * GHOST_HI
        for m, k in enumerate(blocks):
            total = pick_rows(product[size * m : size * (m + 1)], high, OWN_HI + GHOST_HI * k, total)
        return total

    def near_chunk(step):
        cols = pl.ds(step * CHUNK, CHUNK)
        acc_n[:, cols] = pick_ghosts(tab_near, NEAR, cols, acc_n[:, cols])

    ghost_table(tab_near, NEAR)
    near_chunk(0)
    ghost_table(tab_far, FAR)

    live_edges = count[0, 0, 0]

    def edge_chunk(step):
        start = step * CHUNK
        cols = pl.ds(start, CHUNK)
        shape = (8, CHUNK)
        row = iota(shape, 0)
        high_n = sel_n[:, cols]
        high_c = sel_c[:, cols]
        other = pick_ghosts(tab_far, FAR, cols, acc_n[:, cols])
        other = join_rows(other)
        centre = join_rows(acc_c[:, cols])
        block = (high_n - OWN_HI) // GHOST_HI
        cell = block + (block >= 4).astype(jnp.int32)
        third = (cell * 11) >> 5
        side = jnp.where(row & 3 == 0, third - 1, jnp.where(row & 3 == 1, cell - 3 * third - 1, 0))
        side = jnp.where(high_n < OWN_HI, 0, side)
        delta = other - centre + BOX_SIDE * side.astype(F32)
        square = jnp.sum(jnp.where(row < 3, delta * delta, 0.0), axis=0, keepdims=True) + 1.0
        q = tall(jnp.sqrt(square), 8)
        inv_q = 1.0 / q
        freq = (row + 1).astype(F32)
        phase = freq * q
        turn = jnp.floor(phase + 0.5)
        x = (phase - turn) * (jnp.pi / 2)
        x2 = x * x
        sine = x * (1.0 + x2 * (-1.0 / 6 + x2 * (1.0 / 120 + x2 * (-1.0 / 5040 + x2 * (1.0 / 362880)))))
        cosine = 1.0 + x2 * (-0.5 + x2 * (1.0 / 24 + x2 * (-1.0 / 720 + x2 * (1.0 / 40320))))
        quarter = turn.astype(jnp.int32)
        odd = (quarter & 1) == 1
        sign = (1 - (quarter & 2)).astype(F32)
        sin_p = jnp.where(odd, cosine, sine) * sign
        cos_p = jnp.where(odd, -sine, cosine) * sign
        radial = sin_p * inv_q
        kind_c = tall(centre[3:4], 8)
        kind_n = tall(other[3:4], 8)
        kinds = row.astype(F32)
        features = jnp.concatenate(
            [radial, (kind_c == kinds).astype(F32), (kind_n == kinds).astype(F32), jnp.zeros(shape, F32)], axis=0
        ).astype(BF16)

        def active(half):
            t = jnp.tanh(half)
            a = (half + half * t).astype(BF16)
            t = t.astype(BF16)
            return a, (1.0 + t) + a * (1.0 - t)

        act_0, slope_0 = active(dot(w_in, features))
        act_1, slope_1 = active(dot(half_mid[0], act_0))
        act_2, slope_2 = active(dot(half_mid[1], act_1))
        cot_1 = dot(back_1, slope_2).astype(BF16) * slope_1
        cot_0 = dot(back_0, cot_1).astype(BF16) * slope_0
        grad = dot(back_in_w, cot_0)
        pull = grad * ((jnp.pi / 2) * freq * cos_p - radial) * inv_q
        pull = tall(jnp.sum(pull, axis=0, keepdims=True), 8) * inv_q
        live = (start + iota(shape, 1) < live_edges).astype(F32)
        slopes = delta * pull * live
        return slopes, act_2, live, sixteen(high_c.astype(F32)), sixteen(high_n.astype(F32))

    slopes, act_2, live, high_c16, high_n16 = edge_chunk(0)

    backs = [remote(back.at[k], back_in.at[k], 8 + k, *OFFSETS[k]) for k in range(8)]
    slopes16 = spread_rows(-slopes)
    for blocks in (FAR, NEAR):
        ghost_sum = dot_nt(masked_rows(high_n16, slopes16, [OWN_HI + GHOST_HI * k for k in blocks]), hot_n[...])
        for m, k in enumerate(blocks):
            for r in range(3):
                back[k, r] = ghost_sum[16 * m + 4 * r : 16 * m + 4 * r + 4]
        for k in blocks:
            backs[k].start()

    inverse = jnp.zeros((1, ATOMS), F32)
    for kind in range(5):
        inverse = jnp.where(spec_row == float(kind), 1.0 / jnp.full((1, ATOMS), mass[kind], F32), inverse)
    step_row = TIME_STEP * inverse
    step_ref[...] = tall(step_row, 8)
    for r in range(3):
        speeds[r : r + 1, :] = vel[0, r]
        speeds[r + 4 : r + 5, :] = vel[0, r]
    speeds[3:4, :] = step_row
    speeds[7:8, :] = step_row
    state[...] = jnp.zeros(state.shape, F32)
    state[6:7, :] = spec_row
    lists[...] = jnp.zeros(lists.shape, jnp.int32)
    lists[:, 0:MIG] = mig_list[0, 0]
    listed = lists[...]
    moved = pltpu.roll(listed, MIG, 1)
    lane = iota((1, 2 * MIG), 1)
    mig_place = []
    mig_high = []
    mig_shift = []
    mig_valid = []
    for pair in range(4):
        place = jnp.where(lane < MIG, listed[2 * pair : 2 * pair + 1], moved[2 * pair + 1 : 2 * pair + 2])
        write_onehot(hot_m, pl.ds(2 * MIG * pair, 2 * MIG), place & (LO - 1), rows_ref)
        mig_place.append(place)
        mig_high.append(place // LO)
        limit = jnp.where(lane < MIG, mig_count[0, 0, 2 * pair], mig_count[0, 0, 2 * pair + 1] + MIG)
        mig_valid.append((lane < limit).astype(F32))
        row = iota((8, 2 * MIG), 0)
        half = iota((8, 2 * MIG), 1) < MIG
        (a0, b0), (a1, b1) = OFFSETS[2 * pair], OFFSETS[2 * pair + 1]
        mig_shift.append(
            jnp.where(row == 0, jnp.where(half, -BOX_SIDE * a0, -BOX_SIDE * a1), 0.0)
            + jnp.where(row == 1, jnp.where(half, -BOX_SIDE * b0, -BOX_SIDE * b1), 0.0)
        )
    mig_place = jnp.concatenate(mig_place, axis=1)
    mig_high = jnp.concatenate(mig_high, axis=1)
    mig_shift = jnp.concatenate(mig_shift, axis=1)
    mig_valid = jnp.concatenate(mig_valid, axis=1)
    leaving = masked_rows(
        tall(mig_high, 16).astype(F32).astype(BF16), tall(mig_valid, 16).astype(BF16), (0, 4)
    )
    left = dot_nt(leaving, hot_m[...])
    for h in range(OWN_HI):
        at = 16 * (h // 4) + h % 4
        gone[:, LO * h : LO * (h + 1)] = tall(left[at : at + 1], 8)

    mig_high8 = tall(mig_high, 8)

    def leave(table):
        return join_rows(pick_rows(dot(table, hot_m[...]), mig_high8, 0, jnp.zeros((8, 8 * MIG), F32)))

    mig_pos = leave(tab_own[...])
    mig_speed = leave(table_of(split_rows(speeds[...])))
    mig_step = tall(mig_speed[3:4], 8)
    mig_kind = tall(mig_pos[3:4], 8)
    lent_column = tall(lent.astype(F32), 8).T[:, 0:1]
    hot_l[...] = (lent_column == mig_place.astype(F32)).astype(F32).astype(BF16)

    energy = dot(out_rows, act_2) * live
    values16 = spread_rows(jnp.where(iota(slopes.shape, 0) == 3, energy, slopes))
    sum_c = dot_nt(masked_rows(high_c16, values16, (0, 4)), hot_c[...])
    own_sum = sum_c + dot_nt(masked_rows(high_n16, slopes16, (0, 4)), hot_n[...])
    for h in range(OWN_HI):
        span = slice(LO * h, LO * (h + 1))
        at = 16 * (h // 4) + h % 4
        energy_out[0, :, span] = sum_c[at + 12 : at + 13]
        for r in range(4):
            own[r : r + 1, span] = own_sum[at + 4 * r : at + 4 * r + 1]
            own[r + 4 : r + 5, span] = own_sum[at + 4 * r : at + 4 * r + 1]
    mig_force = leave(table_of(split_rows(own[...])))

    total[...] = jnp.zeros(total.shape, F32)
    returned = jnp.zeros((3, GHOST_HI, LO), F32)
    for k in NEAR + FAR:
        backs[k].wait_recv()
        returned = returned + back_in[k]
    for r in range(3):
        for c in range(GHOST_HI):
            span = slice(LO * c, LO * (c + 1))
            total[r : r + 1, span] = returned[r, c : c + 1]
            total[r + 4 : r + 5, span] = returned[r, c : c + 1]
    halves = split_rows(total[...])

    row = iota((8, 8 * MIG), 0)
    mig_force = mig_force + join_rows(dot(sixteen(halves), hot_l[...])[0:8])
    mig_speed = mig_speed + mig_force * mig_step
    mig_pos = mig_pos + TIME_STEP * mig_speed
    carried = jnp.where(row < 3, mig_pos, jnp.where(row < 6, pltpu.roll(mig_speed, 3, 0), mig_kind))
    empty = jnp.where(iota((8, 1), 0) == 6, -1.0, 0.0)
    carried = jnp.where(tall(mig_valid, 8) > 0.0, carried + mig_shift, empty)
    for pair in range(4):
        mig_out[pair] = carried[:, 2 * MIG * pair : 2 * MIG * (pair + 1)]
    moves = [remote(mig_out.at[k // 2], mig_in.at[k], 16 + k, *OFFSETS[k]) for k in range(8)]
    for k in FAR + (3, 4, 1, 6):
        moves[k].start()

    lent_high16 = sixteen(lent_high.astype(F32))
    added = dot_nt(
        jnp.concatenate(
            [masked_rows(lent_high16, spread_rows(doubled(part)), (0, 4)) for part in (halves[0:4], halves[4:8])], axis=0
        ),
        hot_g[...],
    )
    added = added[0 : 4 * OWN_HI] + added[4 * OWN_HI :]
    for h in range(OWN_HI):
        span = slice(LO * h, LO * (h + 1))
        at = 16 * (h // 4) + h % 4
        for r in range(3):
            force_row = own[r : r + 1, span] + added[at + 4 * r : at + 4 * r + 1]
            force_out[0, r, :, span] = force_row
            own[r : r + 1, span] = force_row
        force = own[0:3, span]
        speed = speeds[0:3, span] + force * step_ref[0:3, span]
        state[0:3, span] = pay[0:3, span] + TIME_STEP * speed
        state[3:6, span] = speed
    kept = jnp.where(gone[...] > 0.0, empty, state[...])
    for r in range(7):
        state_out[0, r, :, 0:ATOMS] = kept[r : r + 1]
    for copy in moves:
        copy.wait_recv()
    for pair in range(4):
        arrived = jnp.where(iota((8, 2 * MIG), 1) < MIG, mig_in[2 * pair], mig_in[2 * pair + 1])
        for r in range(7):
            state_out[0, r, :, ATOMS + 2 * MIG * pair : ATOMS + 2 * MIG * (pair + 1)] = arrived[r : r + 1]
    for copy in lends + backs + moves:
        copy.wait_send()


def hand_over(energy, forces, new_state, energy_out, force_out, state_out, sem):
    copies = [
        pltpu.make_async_copy(source, target, sem.at[n])
        for n, (source, target) in enumerate(((energy, energy_out), (forces, force_out), (new_state, state_out)))
    ]
    for copy in copies:
        copy.start()
    for copy in copies:
        copy.wait()


def shards(
    positions, velocities, species, masses, centers, neighbours, edge_count, ghost_list, mig_list, mig_count,
    w_rbf, embed_center, embed_neighbour, w_mid, w_out,
):
    vmem = pl.BlockSpec(memory_space=pltpu.VMEM)
    hbm = pl.BlockSpec(memory_space=pltpu.HBM)
    rows_first = functools.partial(jnp.transpose, axes=(0, 2, 1, 3))
    arguments = (
        rows_first(positions), rows_first(velocities), species, masses, centers, neighbours, edge_count.reshape(1, 1, 1), ghost_list,
        mig_list, mig_count, w_rbf.T, embed_center.T, embed_neighbour.T, w_mid, w_out.reshape(1, -1),
    )
    scalars = (3, 6, 9)
    local = [
        (pltpu.SMEM if n in scalars else pltpu.VMEM)(value.shape, value.dtype) for n, value in enumerate(arguments)
    ]
    energy, forces, new_state = pl.pallas_call(
        functools.partial(kernel, lax.axis_size("gx"), lax.axis_size("gy")),
        out_shape=(
            pltpu.VMEM((1, 1, ATOMS), F32),
            pltpu.VMEM((1, 3, 1, ATOMS), F32),
            pltpu.VMEM((1, 7, 1, ATOMS + 8 * MIG), F32),
        ),
        in_specs=[hbm] * 15,
        out_specs=(vmem, vmem, vmem),
        scratch_shapes=local
        + [
            pltpu.VMEM((LO, max(CHUNK, GHOSTS)), BF16),
            pltpu.VMEM((8, ATOMS), F32),
            pltpu.VMEM((8 * OWN_HI, LO), BF16),
            pltpu.VMEM((32 * GHOST_HI, LO), BF16),
            pltpu.VMEM((32 * GHOST_HI, LO), BF16),
            pltpu.VMEM((LO, EDGES), BF16),
            pltpu.VMEM((LO, EDGES), BF16),
            pltpu.VMEM((LO, GHOSTS), BF16),
            pltpu.VMEM((LO, 8 * MIG), BF16),
            pltpu.VMEM((GHOSTS, 8 * MIG), BF16),
            pltpu.VMEM((8, EDGES), jnp.int32),
            pltpu.VMEM((8, EDGES), jnp.int32),
            pltpu.VMEM((8, EDGES), F32),
            pltpu.VMEM((8, EDGES), F32),
            pltpu.VMEM((4, GHOSTS), F32),
            pltpu.VMEM((8, 4, GHOSTS), F32),
            pltpu.VMEM((8, 3, GHOST_HI, LO), F32),
            pltpu.VMEM((8, 3, GHOST_HI, LO), F32),
            pltpu.VMEM((8, GHOSTS), F32),
            pltpu.VMEM((8, ATOMS), F32),
            pltpu.VMEM((8, ATOMS), F32),
            pltpu.VMEM((8, ATOMS), F32),
            pltpu.VMEM((8, ATOMS), F32),
            pltpu.VMEM((8, 2 * MIG), jnp.int32),
            pltpu.VMEM((4, 8, 2 * MIG), F32),
            pltpu.VMEM((8, 8, 2 * MIG), F32),
            pltpu.VMEM((8, ATOMS), F32),
            pltpu.SemaphoreType.DMA((24,)),
            pltpu.SemaphoreType.DMA((24,)),
            pltpu.SemaphoreType.DMA((15,)),
        ],
        compiler_params=pltpu.CompilerParams(
            collective_id=0, has_side_effects=True, vmem_limit_bytes=60 * 1024 * 1024
        ),
    )(*arguments)
    results = pl.pallas_call(
        hand_over,
        out_shape=tuple(jax.ShapeDtypeStruct(value.shape, F32) for value in (energy, forces, new_state)),
        in_specs=[vmem] * 3,
        out_specs=(hbm, hbm, hbm),
        scratch_shapes=[pltpu.SemaphoreType.DMA((3,))],
    )(*(pltpu.with_memory_space_constraint(value, pltpu.VMEM) for value in (energy, forces, new_state)))
    return (results[0], rows_first(results[1]), rows_first(results[2]))


def solution(mesh):
    return jax.shard_map(
        shards,
        mesh=mesh,
        in_specs=(
            P("gx", "gy", None, None),
            P("gx", "gy", None, None),
            P("gx", "gy", None),
            P(),
            P("gx", "gy", None),
            P("gx", "gy", None),
            P("gx", "gy"),
            P("gx", "gy", None),
            P("gx", "gy", None, None),
            P("gx", "gy", None),
            P(),
            P(),
            P(),
            P(),
            P(),
        ),
        out_specs=(P("gx", "gy", None), P("gx", "gy", None, None), P("gx", "gy", None, None)),
        check_vma=False,
    )
```
